256 devices in a mesh: ctx: 16 (over y, x), head: 8 (over z), pipe: 2 (over core).
Axes of the slice: x: 4, y: 4, z: 8, core: 2. Of those that a mesh axis runs over, the one named last changes fastest.
Arguments:
- queries: bfloat16 [2, 2048, 8192], P('pipe', 'ctx', 'head'), may hold values from -6 to 6
- keys: bfloat16 [2, 2048, 8192], P('pipe', 'ctx', 'head'), may hold values from -6 to 6
- values: bfloat16 [2, 2048, 8192], P('pipe', 'ctx', 'head'), may hold values from -6 to 6
- gates: bfloat16 [2, 2048, 8192], P('pipe', 'ctx', 'head'), may hold values from -6 to 6
- log_decay: float32 [2, 2048, 64], P('pipe', 'ctx', 'head'), may hold values from -1 to 0
- segment_ids: int32 [2, 2048], P('pipe', 'ctx'), may hold values from 0 to 7, never falling along the last dimension, each value on 1 to 512 neighbouring positions
- norm_gain: float32 [2, 8192], P('pipe', 'head'), may hold values from 0.1 to 1.9
- out_weight: bfloat16 [2, 8192, 6144], P('pipe', 'head', 'ctx'), may hold values from -0.0625 to 0.0625
Outputs:
- handed: bfloat16 [2, 2048, 6144], P('pipe', 'ctx', 'head')
The draws below stay inside these ranges and needn't reach their ends.
Inputs may be any that keep to these rules, and one draw needn't show every extreme that they name: `segment_ids`: along each section's tokens the ids never fall; a document has at most a quarter of 2048 tokens, and one has exactly that many.
All inputs are finite; a program needn't handle non-finite values.
Results may differ from the reference program's by a relative error of at most 0.02.
Values may be sent and summed in bfloat16 or wider, within the bound.
A program may use at most 64 MiB of HBM per device.

```python
import math
import jax
import jax.numpy as jnp
import numpy as np
from jax import lax

D = 6144
DH = 128
HEADS = 64
TOK_DEV = 128
TOKENS = 2048
SECTIONS = 2
N_HEAD = 8


def draw_log_decay(key, part):
    streams = jax.random.split(key, 6)
    head_shape = (SECTIONS, 1, HEADS)
    slow_share = 0.5
    chooser = jax.random.uniform(streams[0], head_shape)
    slow_rate = jnp.exp(jax.random.uniform(streams[1], head_shape, minval=math.log(0.2), maxval=math.log(1.0))) / TOKENS
    fast_rate = jnp.exp(jax.random.uniform(streams[2], head_shape, minval=math.log(1.0 / 50.0), maxval=math.log(1.0 / 30.0)))
    base_rate = jnp.where(chooser < slow_share, slow_rate, fast_rate)
    shard_factor = jnp.exp(jax.random.uniform(streams[3], (SECTIONS, TOKENS // TOK_DEV, 1, HEADS), minval=-0.7, maxval=0.7))
    shard_factor = jnp.broadcast_to(shard_factor, (SECTIONS, TOKENS // TOK_DEV, TOK_DEV, HEADS)).reshape(SECTIONS, TOKENS, HEADS)
    token_factor = jnp.exp(jax.random.uniform(streams[4], (SECTIONS, TOKENS, HEADS), minval=-0.7, maxval=0.7))
    rates = base_rate * shard_factor * token_factor
    spots = jax.random.randint(streams[5], (SECTIONS, 2), 0, TOKENS)
    hits = jnp.any(jnp.arange(TOKENS)[None, :, None] == spots[:, None, :], axis=2)
    drops = jnp.log(jax.random.uniform(jax.random.fold_in(key, 7), (SECTIONS, TOKENS, HEADS), minval=0.5, maxval=0.8))
    return jnp.where(hits[:, :, None], drops - rates, -rates).astype(jnp.float32)


def block_levels(stream_key, extent, cuts, least, high):
    loudness, own = 1.0, jax.random.fold_in(stream_key, 6)
    for position, shards_of in cuts:
        heights = jnp.exp(jax.random.uniform(jax.random.fold_in(own, position), (shards_of,), jnp.float32, least / len(cuts), high / len(cuts)))
        loudness = loudness * jnp.repeat(heights, extent[position] // shards_of).reshape([-1 if axis == position else 1 for axis in range(len(extent))])
    return loudness


def split_up(number_of, total, most, slope):
    loads = [(1 << 20) // math.isqrt(rank ** slope) + 1 for rank in range(2, number_of + 1)]
    surplus, given = total - most - (number_of - 1), [1] * (number_of - 1)
    while surplus > 0:
        free = [i for i in range(number_of - 1) if given[i] < most]
        mass, budget = sum([loads[i] for i in free]), surplus
        for i in free:
            extra = min(most - given[i], max(1, budget * loads[i] // mass), surplus)
            given[i] = given[i] + extra
            surplus = surplus - extra
    return np.array([most] + given)


def uneven(stream_key, amount, total, reach, skew):
    if amount == 2:
        one = jax.random.randint(stream_key, (), max(1, total - reach), min(reach, total - 1) + 1)
        return jnp.stack([one, total - one])
    sizes = jnp.asarray(split_up(amount, total, reach, skew), jnp.int32)
    couples = (amount - 1) // 2
    source_of, sink = sizes[1:1 + 2 * couples:2], sizes[2:2 + 2 * couples:2]
    margin = jnp.minimum(source_of - 1, reach - sink)
    shifted = jax.random.randint(jax.random.fold_in(stream_key, 1), (couples,), 0, 1 << 20) % (margin + 1)
    sizes = sizes.at[1:1 + 2 * couples:2].set(source_of - shifted).at[2:2 + 2 * couples:2].set(sink + shifted)
    return sizes[jax.random.permutation(jax.random.fold_in(stream_key, 2), amount)]


def normal_values(rng, shape, deviation, reach, cuts=(), kind=jnp.bfloat16):
    factor_of = block_levels(rng, shape, cuts, -0.22, 0.18) if cuts else 1.0
    values = jax.random.normal(rng, shape, jnp.float32) * deviation * factor_of
    return jnp.minimum(jnp.maximum(values, -reach), reach).astype(kind)


def setup_inputs(seed: int = 0) -> dict:
    splits = jax.random.split(jax.random.key(seed), 9)
    queries = normal_values(splits[0], (SECTIONS, TOKENS, HEADS * DH), 1.0, 6.0, ((0, 2), (1, 16), (2, 8)))
    keys = normal_values(splits[1], (SECTIONS, TOKENS, HEADS * DH), 1.0, 6.0, ((0, 2), (1, 16), (2, 8)))
    values = normal_values(splits[2], (SECTIONS, TOKENS, HEADS * DH), 1.0, 6.0, ((0, 2), (1, 16), (2, 8)))
    gates = normal_values(splits[3], (SECTIONS, TOKENS, HEADS * DH), 1.5, 6.0, ((0, 2), (1, 16), (2, 8)))
    log_decay = draw_log_decay(jax.random.fold_in(splits[8], 71), 0)
    segment_ids = jax.vmap(lambda own: jnp.searchsorted(jnp.cumsum(uneven(own, 8, TOKENS, TOKENS // 4, 2)), jnp.arange(TOKENS), side="right"))(jax.random.split(splits[5], SECTIONS)).reshape((SECTIONS, TOKENS)).astype(jnp.int32)
    norm_gain = jnp.clip(1.0 + 0.18 * jax.random.normal(splits[6], (SECTIONS, HEADS * DH), jnp.float32), 0.1, 1.9)
    out_weight = normal_values(splits[7], (SECTIONS, HEADS * DH, D), (HEADS * DH) ** -0.5, 0.0625, ((0, 2), (1, 8), (2, 16)))
    return dict(queries=queries, keys=keys, values=values, gates=gates, log_decay=log_decay, segment_ids=segment_ids, norm_gain=norm_gain, out_weight=out_weight)


highest = lax.Precision.HIGHEST

def block_step(carried, pieces):
    kv_state, doc_id = carried
    query_rows, key_rows, value_rows, rate_rows, doc_rows = pieces
    length = doc_rows.shape[0]
    running = jnp.cumsum(rate_rows, axis=0)
    running_t = running.T
    causal = lax.broadcasted_iota(jnp.int32, (length, length), 0) >= lax.broadcasted_iota(jnp.int32, (length, length), 1)
    allowed = causal & (doc_rows[:, None] == doc_rows[None, :])
    log_gaps = running_t[:, :, None] - running_t[:, None, :]
    weights = jnp.where(allowed[None], jnp.exp(jnp.where(allowed[None], log_gaps, 0.0)), 0.0)
    scores = jnp.einsum('ihd,jhd->hij', query_rows, key_rows, preferred_element_type=jnp.float32)
    mixed = (scores * weights).astype(jnp.bfloat16)
    inside = jnp.einsum('hij,jhd->ihd', mixed, value_rows, preferred_element_type=jnp.float32)
    query_full = query_rows.astype(jnp.float32)
    key_full = key_rows.astype(jnp.float32)
    value_full = value_rows.astype(jnp.float32)
    reaches = jnp.exp(running) * (doc_rows == doc_id).astype(jnp.float32)[:, None]
    carried_part = jnp.einsum('ihd,hde->ihe', query_full * reaches[:, :, None], kv_state, precision=highest)
    final_doc = doc_rows[-1]
    retain = (doc_id == final_doc).astype(jnp.float32)
    fading = jnp.exp(running[-1][None, :] - running) * (doc_rows == final_doc).astype(jnp.float32)[:, None]
    fresh_part = jnp.einsum('jhd,jhe->hde', key_full * fading[:, :, None], value_full, precision=highest)
    new_state = retain * jnp.exp(running[-1])[:, None, None] * kv_state + fresh_part
    return ((new_state, final_doc), inside + carried_part)

def section_layer(query_rows, key_rows, value_rows, gate_rows, rate_rows, doc_ids, gain_row, weight_rows):
    block_len = min(512, TOK_DEV)
    block_count = TOKENS // block_len
    pieces = (query_rows.reshape(block_count, block_len, HEADS, DH), key_rows.reshape(block_count, block_len, HEADS, DH), value_rows.reshape(block_count, block_len, HEADS, DH), rate_rows.reshape(block_count, block_len, HEADS), doc_ids.astype(jnp.float32).reshape(block_count, block_len))
    start_carry = (jnp.zeros((HEADS, DH, DH), jnp.float32), jnp.array(-1.0, jnp.float32))
    finished, attended = lax.scan(block_step, start_carry, pieces)
    attended = attended.reshape(TOKENS, HEADS, DH)
    scaling = lax.rsqrt(lax.optimization_barrier(jnp.mean(attended * attended, axis=-1, keepdims=True)) + 1e-06)
    normed = ((attended * scaling).reshape(TOKENS, HEADS * DH) * gain_row[None, :] * jax.nn.sigmoid(gate_rows.astype(jnp.float32))).astype(jnp.bfloat16)
    group_width = HEADS * DH // N_HEAD
    summed = jnp.zeros((TOKENS, D), jnp.float32)
    for group_index in range(N_HEAD):
        lower = group_index * group_width
        partial_value = jnp.dot(normed[:, lower:lower + group_width], weight_rows[lower:lower + group_width], preferred_element_type=jnp.float32)
        rounded = lax.optimization_barrier(partial_value.astype(jnp.bfloat16))
        summed = summed + rounded.astype(jnp.float32)
    return summed.astype(jnp.bfloat16)

def reference(queries, keys, values, gates, log_decay, segment_ids, norm_gain, out_weight):
    outputs = []
    for section_index in range(SECTIONS):
        outputs.append(section_layer(queries[section_index], keys[section_index], values[section_index], gates[section_index], log_decay[section_index], segment_ids[section_index], norm_gain[section_index], out_weight[section_index]))
    return jnp.roll(jnp.stack(outputs), 1, axis=0)
```

```python
import jax
import jax.numpy as jnp
from jax import lax
from jax.experimental import pallas as pl
from jax.experimental.pallas import tpu as pltpu
from jax.sharding import PartitionSpec as P

MESH = pl.DeviceIdType.MESH
F32 = jnp.float32
BF16 = jnp.bfloat16
HIGHEST = lax.Precision.HIGHEST

DH = 128
TOK = 128
ROW = 512
HW = 256
KD = 1024
NW = 384
SH = 64
DELTAS = (1, 3, 2)


def dot(a, b, dims=((1,), (0,)), precision=None):
    return lax.dot_general(
        a, b, (dims, ((), ())), precision=precision, preferred_element_type=F32
    )


def kernel(
    k_hbm, v_hbm, q_hbm, g_hbm, pk_ref, gain_ref, w_hbm, out_hbm,
    rx, pkx, kf, att, abuf, wbuf, st_out, st_in, pbuf, rl, rs, fin,
    lsem, wlsem, a2a_s, a2a_r, pk_s, pk_r, w_s, w_r, wr_s, wr_r, st_sem,
    ag_s, ag_r, agr_s, agr_r, rl_s, rl_r, rs_s, rs_r, fin_s, fin_r,
):
    c, z, p = lax.axis_index("ctx"), lax.axis_index("head"), lax.axis_index("pipe")
    x, y = lax.rem(c, 4), lax.div(c, 4)

    def at_x(d):
        return 4 * y + lax.rem(x + d, 4)

    def at_y(d):
        return 4 * lax.rem(y + d, 4) + x

    def at_z(d):
        return lax.rem(z + d + 8, 8)

    def remote(src, dst, send, recv, dev):
        return pltpu.make_async_remote_copy(
            src_ref=src, dst_ref=dst, send_sem=send, recv_sem=recv,
            device_id=dev, device_id_type=MESH,
        )

    def arrived(dst, recv):
        remote(dst, dst, recv, recv, (c, z, 1 - p)).wait_recv()

    sent = []

    def send(*a):
        copy = remote(*a)
        copy.start()
        sent.append(copy)

    local = []
    for a, ref in enumerate((k_hbm, v_hbm, q_hbm, g_hbm)):
        cp = pltpu.make_async_copy(
            ref.at[0, :, pl.ds(pl.multiple_of(x * HW, HW), HW)],
            rx.at[a, pl.ds(pl.multiple_of(x * TOK, TOK), TOK), :],
            lsem.at[a],
        )
        cp.start()
        local.append(cp)
    w_local = pltpu.make_async_copy(w_hbm.at[0], wbuf.at[0], wlsem)
    w_local.start()

    fin_ctx = 4 * y + lax.div(z, 2)

    def fin_head(yy):
        return 2 * yy + lax.div(x, 2)

    def phase_y(ph):
        return lax.rem(y + (0, 3, 1, 2)[ph], 4)

    barrier = pltpu.get_barrier_semaphore()
    peers = [(at_x(d), z, p) for d in DELTAS]
    peers += [(at_y(1), z, p), (at_y(3), z, p)]
    peers += [(c, at_z(1), p), (c, at_z(-1), p)]
    peers += [(fin_ctx, fin_head(yy), 1 - p) for yy in range(4)]
    for zz in range(2):
        for xx in range(2):
            peers.append(
                (4 * lax.div(z, 2) + 2 * lax.rem(z, 2) + xx, 2 * x + zz, 1 - p)
            )
    for dev in peers:
        pl.semaphore_signal(barrier, inc=1, device_id=dev, device_id_type=MESH)
    pl.semaphore_wait(barrier, len(peers))

    for i, d in enumerate(DELTAS):
        to = lax.rem(x + d, 4)
        send(pk_ref.at[to], pkx.at[x], pk_s.at[i], pk_r.at[i], (at_x(d), z, p))

    def a2a(a, ref):
        for i, d in enumerate(DELTAS):
            to = lax.rem(x + d, 4)
            send(
                ref.at[0, :, pl.ds(pl.multiple_of(to * HW, HW), HW)],
                rx.at[a, pl.ds(pl.multiple_of(x * TOK, TOK), TOK), :],
                a2a_s.at[a, i], a2a_r.at[a, i], (at_x(d), z, p),
            )

    def a2a_wait(a):
        for i, d in enumerate(DELTAS):
            src = lax.rem(x + 4 - d, 4)
            arrived(
                rx.at[a, pl.ds(pl.multiple_of(src * TOK, TOK), TOK), :], a2a_r.at[a, i]
            )

    a2a(0, k_hbm)
    a2a(1, v_hbm)
    for i in range(4):
        for side, (d, ch) in enumerate(((1, i), (3, (i + 2) % 4))):
            rows = pl.ds(ch * HW, HW)
            send(
                w_hbm.at[0, rows, :], wbuf.at[1 + side, rows, :],
                w_s.at[side, ch], w_r.at[side, ch], (at_y(d), z, p),
            )
    a2a(2, q_hbm)
    a2a(3, g_hbm)

    def w_wait(side, ch):
        arrived(wbuf.at[1 + side, pl.ds(ch * HW, HW), :], w_r.at[side, ch])

    def w_relay(side, ch):
        rows = pl.ds(ch * HW, HW)
        send(
            wbuf.at[1 + side, rows, :], wbuf.at[3, rows, :],
            wr_s.at[ch], wr_r.at[ch], (at_y((1, 3)[side]), z, p),
        )

    for i, d in enumerate(DELTAS):
        arrived(pkx.at[lax.rem(x + 4 - d, 4)], pk_r.at[i])
    pkx[x] = pk_ref[x]
    ia = lax.broadcasted_iota(jnp.int32, (TOK, TOK), 0)
    ib = lax.broadcasted_iota(jnp.int32, (TOK, TOK), 1)
    upper = (ia <= ib).astype(F32)
    lower = (ia >= ib).astype(F32)
    eye = (ia == ib).astype(F32)
    rows_, cols_, segr, segc = [], [], [], []
    off_r, off_c = jnp.zeros((8, 1), F32), jnp.zeros((1, 8), F32)
    for b in range(4):
        part = pkx[b]
        r = dot(part, upper, precision=HIGHEST) + off_r
        s = dot(lower, part, ((1,), (1,)), precision=HIGHEST) + off_c
        e = dot(eye, part, ((1,), (1,)), precision=HIGHEST)
        off_r, off_c = r[:, TOK - 1 : TOK], s[TOK - 1 : TOK, :]
        rows_.append(r)
        cols_.append(s)
        segr.append(part[2:3, :])
        segc.append(e[:, 2:3])
    last_doc = segr[3][:, TOK - 1 : TOK]

    local[0].wait()
    local[1].wait()
    a2a_wait(0)
    a2a_wait(1)
    for b in range(4):
        keep = (segc[b] == last_doc).astype(F32)
        rr = pl.ds(b * TOK, TOK)
        for h in range(2):
            fade = jnp.exp(jnp.minimum(off_c[:, h : h + 1] - cols_[b][:, h : h + 1], 0.0)) * keep
            hh = slice(h * DH, (h + 1) * DH)
            kf[rr, hh] = (rx[0, rr, hh].astype(F32) * fade).astype(BF16)
    for h in range(2):
        hh = slice(h * DH, (h + 1) * DH)
        st_out[hh, :] = dot(kf[:, hh], rx[1, :, hh], ((0,), (0,))).astype(BF16)
    st_out[256:272, :] = jnp.broadcast_to(last_doc, (16, DH)).astype(BF16)
    send(st_out, st_in, st_sem.at[0], st_sem.at[1], (at_y(1), z, p))

    local[2].wait()
    a2a_wait(2)
    for i in range(4):
        n = (i + 1) * TOK
        rr = pl.ds(i * TOK, TOK)
        seg_row = jnp.concatenate(segr[: i + 1], axis=1)
        it = lax.broadcasted_iota(jnp.int32, (TOK, n), 0) + i * TOK
        ij = lax.broadcasted_iota(jnp.int32, (TOK, n), 1)
        allowed = (ij <= it) & (segc[i] == seg_row)
        for h in range(2):
            hh = slice(h * DH, (h + 1) * DH)
            crow = jnp.concatenate([r[h : h + 1, :] for r in rows_[: i + 1]], axis=1)
            gap = jnp.minimum(cols_[i][:, h : h + 1] - crow, 0.0)
            weight = jnp.where(allowed, jnp.exp(gap), 0.0)
            scores = dot(rx[2, rr, hh], rx[0, 0:n, hh], ((1,), (1,)))
            mixed = (scores * weight).astype(BF16)
            att[rr, hh] = dot(mixed, rx[1, 0:n, hh])

    for side in range(2):
        for ch in (0, 1) if side == 0 else (2, 3):
            w_wait(side, ch)
            w_relay(side, ch)

    local[3].wait()
    a2a_wait(3)
    arrived(st_in, st_sem.at[1])
    prev_doc = st_in[256:257, 0:1].astype(F32)
    later = (y > 0).astype(F32)
    for i in range(4):
        rr = pl.ds(i * TOK, TOK)
        same = (segc[i] == prev_doc).astype(F32) * later
        for h in range(2):
            hh = slice(h * DH, (h + 1) * DH)
            reach = jnp.exp(cols_[i][:, h : h + 1]) * same
            full = att[rr, hh] + dot(rx[2, rr, hh], st_in[hh, :]) * reach
            scale = lax.rsqrt(jnp.mean(full * full, axis=-1, keepdims=True) + 1e-06)
            gain = gain_ref[:, pl.ds(pl.multiple_of(x * HW + h * DH, DH), DH)]
            gate = 1.0 / (1.0 + jnp.exp(-rx[3, rr, hh].astype(F32)))
            abuf[0, rr, hh] = (full * scale * gain * gate).astype(BF16)
        for side, d in enumerate((1, 3)):
            send(
                abuf.at[0, rr, :], abuf.at[1 + side, rr, :],
                ag_s.at[side, i], ag_r.at[side, i], (at_x(d), z, p),
            )
    for side in range(2):
        for ch in (0, 1) if side == 0 else (2, 3):
            rr = pl.ds(ch * TOK, TOK)
            arrived(abuf.at[1 + side, rr, :], ag_r.at[side, ch])
            send(
                abuf.at[1 + side, rr, :], abuf.at[3, rr, :],
                agr_s.at[ch], agr_r.at[ch], (at_x((1, 3)[side]), z, p),
            )
    for side in range(2):
        for ch in (2, 3) if side == 0 else (0, 1):
            arrived(abuf.at[1 + side, pl.ds(ch * TOK, TOK), :], ag_r.at[side, ch])
    for ch in range(4):
        arrived(abuf.at[3, pl.ds(ch * TOK, TOK), :], agr_r.at[ch])

    xs = [lax.rem(x + d, 4) for d in (0, 3, 1, 2)]

    def project(ph):
        def body(i, carry):
            rr = pl.ds(pl.multiple_of(i * TOK, TOK), TOK)
            acc = jnp.zeros((TOK, NW), F32)
            for s in range(4):
                kk = pl.ds(pl.multiple_of(xs[s] * HW, HW), HW)
                acc = acc + dot(abuf[s, rr, :], wbuf[ph, kk, :])
            pbuf[ph, rr, :] = acc.astype(BF16)
            return carry

        lax.fori_loop(0, 4, body, 0)

    def share(owner):
        return pl.ds(pl.multiple_of(lax.rem(owner + 16, 8) * SH, SH), SH)

    def long_send(ph, t):
        s = (1, -1)[ph % 2]
        src = pbuf.at[ph, share(z - s * 4), :] if t == 0 else rl.at[ph, t - 1]
        send(src, rl.at[ph, t], rl_s.at[ph, t], rl_r.at[ph, t], (c, at_z(-s), p))

    def short_send(ph, t):
        s = (1, -1)[ph % 2]
        src = pbuf.at[ph, share(z + s * 3), :] if t == 0 else rs.at[ph, t - 1]
        send(src, rs.at[ph, t], rs_s.at[ph, t], rs_r.at[ph, t], (c, at_z(s), p))

    def step(ph, t):
        s = (1, -1)[ph % 2]
        arrived(rl.at[ph, t], rl_r.at[ph, t])
        if t < 3:
            rl[ph, t] = (
                rl[ph, t].astype(F32) + pbuf[ph, share(z - s * (3 - t)), :].astype(F32)
            ).astype(BF16)
            long_send(ph, t + 1)
        if t < 2:
            arrived(rs.at[ph, t], rs_r.at[ph, t])
            rs[ph, t] = (
                rs[ph, t].astype(F32) + pbuf[ph, share(z + s * (2 - t)), :].astype(F32)
            ).astype(BF16)
            short_send(ph, t + 1)
        if t == 3:
            arrived(rs.at[ph, 2], rs_r.at[ph, 2])
            fin[ph] = (
                rl[ph, 3].astype(F32) + rs[ph, 2].astype(F32) + pbuf[ph, share(z), :].astype(F32)
            ).astype(BF16)
            send(
                fin.at[ph],
                out_hbm.at[
                    0,
                    pl.ds(pl.multiple_of(lax.rem(z, 2) * SH, SH), SH),
                    pl.ds(pl.multiple_of(lax.rem(x, 2) * NW, NW), NW),
                ],
                fin_s.at[ph], fin_r.at[lax.rem(z, 2), lax.rem(x, 2)],
                (fin_ctx, fin_head(phase_y(ph)), 1 - p),
            )

    w_local.wait()
    project(0)
    long_send(0, 0)
    short_send(0, 0)
    for side in range(2):
        for ch in (2, 3) if side == 0 else (0, 1):
            w_wait(side, ch)
        project(1 + side)
        long_send(1 + side, 0)
        short_send(1 + side, 0)
    for t in range(4):
        for ph in range(3):
            step(ph, t)
    for ch in range(4):
        arrived(wbuf.at[3, pl.ds(ch * HW, HW), :], wr_r.at[ch])
    project(3)
    long_send(3, 0)
    short_send(3, 0)
    for t in range(4):
        step(3, t)

    for zz in range(2):
        for xx in range(2):
            arrived(
                out_hbm.at[0, pl.ds(zz * SH, SH), pl.ds(xx * NW, NW)], fin_r.at[zz, xx]
            )
    for copy in sent:
        copy.wait_send()


def on_device(queries, keys, values, gates, log_decay, segment_ids, norm_gain, out_weight):
    decay = log_decay[0].T.reshape(4, 2, TOK)
    docs = jnp.broadcast_to(segment_ids.astype(F32)[None], (4, 1, TOK))
    packed = jnp.concatenate([decay, docs, jnp.zeros((4, 5, TOK), F32)], axis=1)
    hbm = pl.BlockSpec(memory_space=pltpu.HBM)
    vmem = pl.BlockSpec(memory_space=pltpu.VMEM)
    dma = pltpu.SemaphoreType.DMA
    return pl.pallas_call(
        kernel,
        out_shape=jax.ShapeDtypeStruct((1, TOK, 2 * NW), BF16),
        in_specs=[hbm, hbm, hbm, hbm, vmem, vmem, hbm],
        out_specs=hbm,
        scratch_shapes=[
            pltpu.VMEM((4, ROW, HW), BF16),
            pltpu.VMEM((4, 8, TOK), F32),
            pltpu.VMEM((ROW, HW), BF16),
            pltpu.VMEM((ROW, HW), F32),
            pltpu.VMEM((4, ROW, HW), BF16),
            pltpu.VMEM((4, KD, NW), BF16),
            pltpu.VMEM((272, DH), BF16),
            pltpu.VMEM((272, DH), BF16),
            pltpu.VMEM((4, ROW, NW), BF16),
            pltpu.VMEM((4, 4, SH, NW), BF16),
            pltpu.VMEM((4, 3, SH, NW), BF16),
            pltpu.VMEM((4, SH, NW), BF16),
            dma((4,)), dma,
            dma((4, 3)), dma((4, 3)), dma((3,)), dma((3,)),
            dma((2, 4)), dma((2, 4)), dma((4,)), dma((4,)), dma((2,)),
            dma((2, 4)), dma((2, 4)), dma((4,)), dma((4,)),
            dma((4, 4)), dma((4, 4)), dma((4, 3)), dma((4, 3)),
            dma((4,)), dma((2, 2)),
        ],
        compiler_params=pltpu.CompilerParams(
            collective_id=0, has_side_effects=True, vmem_limit_bytes=60 * 2**20
        ),
        cost_estimate=pl.CostEstimate(
            flops=2 * 10**9, bytes_accessed=3 * 2**20, transcendentals=10**6
        ),
    )(keys, values, queries, gates, packed, norm_gain, out_weight)


def solution(mesh):
    return jax.shard_map(
        on_device,
        mesh=mesh,
        in_specs=(
            P("pipe", "ctx", "head"),
            P("pipe", "ctx", "head"),
            P("pipe", "ctx", "head"),
            P("pipe", "ctx", "head"),
            P("pipe", "ctx", "head"),
            P("pipe", "ctx"),
            P("pipe", "head"),
            P("pipe", "head", "ctx"),
        ),
        out_specs=P("pipe", "ctx", "head"),
        check_vma=False,
    )
```

```python
import jax
import jax.numpy as jnp
from jax import lax
from jax.experimental import pallas as pl
from jax.experimental.pallas import tpu as pltpu
from jax.sharding import PartitionSpec as P

MESH = pl.DeviceIdType.MESH
F32 = jnp.float32
BF16 = jnp.bfloat16
HIGHEST = lax.Precision.HIGHEST

DH = 128
TOK = 128
HW = 256
KD = 1024
NW = 384
N3 = 3 * NW
CH = 32
SH = 16
DELTAS = (1, 3, 2)


def dot(a, b, dims=((1,), (0,)), precision=None):
    return lax.dot_general(
        a, b, (dims, ((), ())), precision=precision, preferred_element_type=F32
    )


def kernel(
    k_hbm, v_hbm, q_hbm, g_hbm, decay_hbm, docs_hbm, gain_hbm, w_hbm, out_hbm,
    rx, pk, docs, gain, pkx, kf, att, abuf, wbuf, st_out, st_in,
    pa, la, sa, fa, pb, lb, sb, fb,
    lsem, a2a_s, a2a_r, pk_s, pk_r, w_s, w_r, wr_s, wr_r, st_sem,
    ag_s, ag_r, l_s, l_r, s_s, s_r, fin_s, fin_r,
):
    c, z, p = lax.axis_index("ctx"), lax.axis_index("head"), lax.axis_index("pipe")
    x, y = lax.rem(c, 4), lax.div(c, 4)

    def at_x(d):
        return 4 * y + lax.rem(x + d, 4)

    def at_y(d):
        return 4 * lax.rem(y + d, 4) + x

    def at_z(d):
        return lax.rem(z + d + 8, 8)

    def block(i, size):
        return pl.ds(pl.multiple_of(i * size, size), size)

    def remote(src, dst, send, recv, dev):
        return pltpu.make_async_remote_copy(
            src_ref=src, dst_ref=dst, send_sem=send, recv_sem=recv,
            device_id=dev, device_id_type=MESH,
        )

    def arrived(dst, recv):
        remote(dst, dst, recv, recv, (c, z, 1 - p)).wait_recv()

    sent = []

    def send(*a):
        copy = remote(*a)
        copy.start()
        sent.append(copy)

    local = [
        pltpu.make_async_copy(src, dst, lsem.at[i])
        for i, (src, dst) in enumerate(
            [
                (ref.at[0, :, block(x, HW)], rx.at[a, x])
                for a, ref in enumerate((k_hbm, v_hbm, q_hbm, g_hbm))
            ]
            + [
                (decay_hbm, pk.at[0:8, :]),
                (docs_hbm, docs),
                (gain_hbm.at[:, block(x, HW)], gain),
                (w_hbm.at[0], wbuf.at[0]),
            ]
        )
    ]
    for i in (4, 5, 6, 0, 1, 2, 3, 7):
        local[i].start()

    def fin_dev(yy):
        return (4 * y + lax.div(z, 2), 2 * yy + lax.div(x, 2), 1 - p)

    def phase_y(ph):
        return lax.rem(y + (0, 3, 1, 2)[ph], 4)

    barrier = pltpu.get_barrier_semaphore()
    peers = [(at_x(d), z, p) for d in DELTAS]
    peers += [(at_y(1), z, p), (at_y(3), z, p)]
    peers += [(c, at_z(1), p), (c, at_z(-1), p)]
    peers += [fin_dev(yy) for yy in range(4)]
    for zz in range(2):
        for xx in range(2):
            peers.append(
                (4 * y + 2 * lax.rem(z, 2) + xx, 2 * x + zz, 1 - p)
            )
    for dev in peers:
        pl.semaphore_signal(barrier, inc=1, device_id=dev, device_id_type=MESH)
    local[4].wait()
    local[5].wait()
    pk[8:16, :] = jnp.broadcast_to(docs[...].astype(F32), (8, TOK))
    pl.semaphore_wait(barrier, len(peers))

    for i, d in enumerate(DELTAS):
        send(pk, pkx.at[x], pk_s.at[i], pk_r.at[i], (at_x(d), z, p))

    def a2a(a, ref):
        for i, d in enumerate(DELTAS):
            to = lax.rem(x + d, 4)
            send(
                ref.at[0, :, block(to, HW)], rx.at[a, x],
                a2a_s.at[a, i], a2a_r.at[a, i], (at_x(d), z, p),
            )

    def a2a_wait(a):
        local[a].wait()
        for i, d in enumerate(DELTAS):
            arrived(rx.at[a, lax.rem(x + 4 - d, 4)], a2a_r.at[a, i])

    def w_send(side, ch):
        rows = pl.ds(ch * HW, HW)
        send(
            w_hbm.at[0, rows, :], wbuf.at[1 + side, rows, :],
            w_s.at[side, ch], w_r.at[side, ch], (at_y((1, 3)[side]), z, p),
        )

    def w_wait(side, ch):
        arrived(wbuf.at[1 + side, pl.ds(ch * HW, HW), :], w_r.at[side, ch])

    def w_relay(side, ch):
        rows = pl.ds(ch * HW, HW)
        w_wait(side, ch)
        send(
            wbuf.at[1 + side, rows, :], wbuf.at[3, rows, :],
            wr_s.at[ch], wr_r.at[ch], (at_y((1, 3)[side]), z, p),
        )

    a2a(0, k_hbm)
    a2a(1, v_hbm)
    w_send(0, 0)
    w_send(1, 2)
    a2a(2, q_hbm)
    a2a(3, g_hbm)
    w_send(0, 1)
    w_send(1, 3)
    w_send(1, 0)
    w_send(1, 1)

    i8 = lax.broadcasted_iota(jnp.int32, (8, 8), 0)
    j8 = lax.broadcasted_iota(jnp.int32, (8, 8), 1)
    pick = (j8 == 2 * x + i8).astype(F32)
    ia = lax.broadcasted_iota(jnp.int32, (TOK, TOK), 0)
    ib = lax.broadcasted_iota(jnp.int32, (TOK, TOK), 1)
    upper = (ia <= ib).astype(F32)
    lower = (ia >= ib).astype(F32)
    eye = (ia == ib).astype(F32)
    for i, d in enumerate(DELTAS):
        arrived(pkx.at[lax.rem(x + 4 - d, 4)], pk_r.at[i])
    pkx[x] = pk[...]
    rows_, cols_, segr, segc = [], [], [], []
    off_r, off_c = jnp.zeros((8, 1), F32), jnp.zeros((1, 8), F32)
    for b in range(4):
        part = dot(pick, pkx[b, 0:8, :], precision=HIGHEST)
        r = dot(part, upper, precision=HIGHEST) + off_r
        s = dot(lower, part, ((1,), (1,)), precision=HIGHEST) + off_c
        e = dot(eye, pkx[b, 8:16, :], ((1,), (1,)), precision=HIGHEST)
        off_r, off_c = r[:, TOK - 1 : TOK], s[TOK - 1 : TOK, :]
        rows_.append(r)
        cols_.append(s)
        segr.append(pkx[b, 8:9, :])
        segc.append(e[:, 0:1])
    last_doc = segr[3][:, TOK - 1 : TOK]

    a2a_wait(0)
    a2a_wait(1)
    for b in range(4):
        keep = (segc[b] == last_doc).astype(F32)
        for h in range(2):
            hs = slice(h, h + 1)
            hh = slice(h * DH, (h + 1) * DH)
            fade = jnp.exp(jnp.minimum(off_c[:, hs] - cols_[b][:, hs], 0.0)) * keep
            kf[b * TOK : (b + 1) * TOK, hh] = (rx[0, b, :, hh].astype(F32) * fade).astype(BF16)
    for h in range(2):
        hh = slice(h * DH, (h + 1) * DH)
        values = rx[1, :, :, hh].reshape(4 * TOK, DH)
        st_out[hh, :] = dot(kf[:, hh], values, ((0,), (0,))).astype(BF16)
    st_out[256:272, :] = jnp.broadcast_to(last_doc, (16, DH)).astype(BF16)
    send(st_out, st_in, st_sem.at[0], st_sem.at[1], (at_y(1), z, p))
    w_send(0, 2)
    w_send(0, 3)

    a2a_wait(2)
    for i in range(4):
        n = (i + 1) * TOK
        seg_row = jnp.concatenate(segr[: i + 1], axis=1)
        it = lax.broadcasted_iota(jnp.int32, (TOK, n), 0) + i * TOK
        ij = lax.broadcasted_iota(jnp.int32, (TOK, n), 1)
        allowed = (ij <= it) & (segc[i] == seg_row)
        for h in range(2):
            hh = slice(h * DH, (h + 1) * DH)
            crow = jnp.concatenate([r[h : h + 1, :] for r in rows_[: i + 1]], axis=1)
            gap = jnp.minimum(cols_[i][:, h : h + 1] - crow, 0.0)
            weight = jnp.where(allowed, jnp.exp(gap), 0.0)
            key_rows = rx[0, 0 : i + 1, :, hh].reshape(n, DH)
            scores = dot(rx[2, i, :, hh], key_rows, ((1,), (1,)))
            mixed = (scores * weight).astype(BF16)
            att[i, :, hh] = dot(mixed, rx[1, 0 : i + 1, :, hh].reshape(n, DH))

    a2a_wait(3)
    arrived(st_in, st_sem.at[1])
    local[6].wait()
    prev_doc = st_in[256:257, 0:1].astype(F32)
    later = (y > 0).astype(F32)
    for i in range(4):
        same = (segc[i] == prev_doc).astype(F32) * later
        for h in range(2):
            hh = slice(h * DH, (h + 1) * DH)
            reach = jnp.exp(cols_[i][:, h : h + 1]) * same
            full = att[i, :, hh] + dot(rx[2, i, :, hh], st_in[hh, :]) * reach
            scale = lax.rsqrt(jnp.mean(full * full, axis=-1, keepdims=True) + 1e-06)
            gate = 1.0 / (1.0 + jnp.exp(-rx[3, i, :, hh].astype(F32)))
            abuf[0, i, :, hh] = (full * scale * gain[:, hh] * gate).astype(BF16)

    for j in range(4):
        for i, d in enumerate(DELTAS):
            rr = pl.ds(j * CH, CH)
            send(
                abuf.at[0, :, rr, :], abuf.at[1 + i, :, rr, :],
                ag_s.at[i, j], ag_r.at[i, j], (at_x(d), z, p),
            )

    for ch in range(2):
        w_relay(0, ch)
        w_relay(1, 2 + ch)

    xs = [lax.rem(x + d, 4) for d in (0, 3, 1, 2)]
    local[7].wait()

    def project_a(j):
        for i in range(3):
            arrived(abuf.at[1 + i, :, pl.ds(j * CH, CH), :], ag_r.at[i, j])
        if j == 0:
            for ch in range(2):
                w_wait(0, 2 + ch)
                w_wait(1, ch)

        def body(ph, carry):
            acc = jnp.zeros((4 * CH, NW), F32)
            for s in range(4):
                lhs = abuf[s, :, j * CH : (j + 1) * CH, :].reshape(4 * CH, HW)
                acc = acc + dot(lhs, wbuf[ph, block(xs[s], HW), :])
            pa[j, :, block(ph, NW)] = acc.astype(BF16)
            return carry

        lax.fori_loop(0, 3, body, 0)

    def project_b():
        for ch in range(4):
            arrived(wbuf.at[3, pl.ds(ch * HW, HW), :], wr_r.at[ch])

        def body(b, carry):
            acc = jnp.zeros((TOK, NW), F32)
            for s in range(4):
                acc = acc + dot(abuf[s, b], wbuf[3, block(xs[s], HW), :])
            acc = acc.astype(BF16)
            for half in range(2):
                for j in range(4):
                    low = j * CH + half * SH
                    pb[2 * b + half, j] = acc[low : low + SH, :]
            return carry

        lax.fori_loop(0, 4, body, 0)

    def own(b, owner):
        o = lax.rem(owner + 16, 8)
        return pb.at[o] if b == 4 else pa.at[b, block(o, SH), :]

    def longs(b, t):
        return lb.at[t] if b == 4 else la.at[b, t]

    def shorts(b, t):
        return sb.at[t] if b == 4 else sa.at[b, t]

    def sign(b):
        return (1, -1)[b % 2]

    def long_send(b, t):
        s = sign(b)
        src = own(b, z - s * 4) if t == 0 else longs(b, t - 1)
        send(src, longs(b, t), l_s.at[b, t], l_r.at[b, t], (c, at_z(-s), p))

    def short_send(b, t):
        s = sign(b)
        src = own(b, z + s * 3) if t == 0 else shorts(b, t - 1)
        send(src, shorts(b, t), s_s.at[b, t], s_r.at[b, t], (c, at_z(s), p))

    def start(b):
        if b == 4:
            project_b()
        else:
            project_a(b)
        long_send(b, 0)
        short_send(b, 0)

    def step(b, t):
        s = sign(b)
        arrived(longs(b, t), l_r.at[b, t])
        if t < 3:
            ref = longs(b, t)
            mine = own(b, z - s * (3 - t))
            ref[...] = (ref[...].astype(F32) + mine[...].astype(F32)).astype(BF16)
            long_send(b, t + 1)
        if t < 2:
            arrived(shorts(b, t), s_r.at[b, t])
            ref = shorts(b, t)
            mine = own(b, z + s * (2 - t))
            ref[...] = (ref[...].astype(F32) + mine[...].astype(F32)).astype(BF16)
            short_send(b, t + 1)
        if t == 3:
            arrived(shorts(b, 2), s_r.at[b, 2])
            total = longs(b, 3)[...].astype(F32) + shorts(b, 2)[...].astype(F32)
            total = (total + own(b, z)[...].astype(F32)).astype(BF16)
            if b == 4:
                fb[...] = total
            else:
                fa[b] = total
            for n in range(4 if b == 4 else 3):
                j, ph = (n, 3) if b == 4 else (b, n)
                src = fb.at[j] if b == 4 else fa.at[b, :, pl.ds(ph * NW, NW)]
                low = pl.multiple_of(j * CH + lax.rem(z, 2) * SH, SH)
                send(
                    src, out_hbm.at[0, pl.ds(low, SH), block(lax.rem(x, 2), NW)],
                    fin_s.at[j, ph], fin_r.at[j, lax.rem(z, 2), lax.rem(x, 2)],
                    fin_dev(phase_y(ph)),
                )

    for slot in range(9):
        for b in range(5):
            if 0 <= slot - 1 - b < 4:
                step(b, slot - 1 - b)
        if slot < 5:
            start(slot)

    for j in range(4):
        for zz in range(2):
            for xx in range(2):
                arrived(
                    out_hbm.at[0, pl.ds(j * CH + zz * SH, SH), pl.ds(xx * NW, NW)],
                    fin_r.at[j, zz, xx],
                )
    for copy in sent:
        copy.wait_send()


def on_device(queries, keys, values, gates, log_decay, segment_ids, norm_gain, out_weight):
    hbm = pl.BlockSpec(memory_space=pltpu.HBM)
    vmem = pltpu.VMEM
    dma = pltpu.SemaphoreType.DMA
    return pl.pallas_call(
        kernel,
        out_shape=jax.ShapeDtypeStruct((1, TOK, 2 * NW), BF16),
        in_specs=[hbm] * 8,
        out_specs=hbm,
        scratch_shapes=[
            vmem((4, 4, TOK, HW), BF16),
            vmem((16, TOK), F32),
            vmem((1, TOK), jnp.int32),
            vmem((1, HW), F32),
            vmem((4, 16, TOK), F32),
            vmem((4 * TOK, HW), BF16),
            vmem((4, TOK, HW), F32),
            vmem((4, 4, TOK, HW), BF16),
            vmem((4, KD, NW), BF16),
            vmem((272, DH), BF16),
            vmem((272, DH), BF16),
            vmem((4, TOK, N3), BF16),
            vmem((4, 4, SH, N3), BF16),
            vmem((4, 3, SH, N3), BF16),
            vmem((4, SH, N3), BF16),
            vmem((8, 4, SH, NW), BF16),
            vmem((4, 4, SH, NW), BF16),
            vmem((3, 4, SH, NW), BF16),
            vmem((4, SH, NW), BF16),
            dma((8,)), dma((4, 3)), dma((4, 3)), dma((3,)), dma((3,)),
            dma((2, 4)), dma((2, 4)), dma((4,)), dma((4,)), dma((2,)),
            dma((3, 4)), dma((3, 4)),
            dma((5, 4)), dma((5, 4)), dma((5, 3)), dma((5, 3)),
            dma((4, 4)), dma((4, 2, 2)),
        ],
        compiler_params=pltpu.CompilerParams(
            collective_id=0, has_side_effects=True, vmem_limit_bytes=60 * 2**20
        ),
        cost_estimate=pl.CostEstimate(
            flops=2 * 10**9, bytes_accessed=3 * 2**20, transcendentals=10**6
        ),
    )(
        keys, values, queries, gates, log_decay[0].T, segment_ids, norm_gain, out_weight
    )


def solution(mesh):
    return jax.shard_map(
        on_device,
        mesh=mesh,
        in_specs=(
            P("pipe", "ctx", "head"),
            P("pipe", "ctx", "head"),
            P("pipe", "ctx", "head"),
            P("pipe", "ctx", "head"),
            P("pipe", "ctx", "head"),
            P("pipe", "ctx"),
            P("pipe", "head"),
            P("pipe", "head", "ctx"),
        ),
        out_specs=P("pipe", "ctx", "head"),
        check_vma=False,
    )
```

```python
import jax
import jax.numpy as jnp
from jax import lax
from jax.experimental import pallas as pl
from jax.experimental.pallas import tpu as pltpu
from jax.sharding import PartitionSpec as P

MESH = pl.DeviceIdType.MESH
F32 = jnp.float32
BF16 = jnp.bfloat16
HIGHEST = lax.Precision.HIGHEST

DH = 128
TOK = 128
HW = 256
KD = 1024
NW = 384
CH = 32
SH = 64
DELTAS = (1, 3, 2)
ORDER = (
    ("S", 0), ("S", 1), ("S", 2), ("S", 3), ("L",), ("T", 0, 0),
    ("U", 0, 0), ("T", 1, 0), ("U", 1, 0), ("T", 2, 0), ("U", 2, 0), ("T", 3, 0),
    ("U", 3, 0), ("T", 0, 1), ("U", 0, 1), ("T", 1, 1), ("U", 1, 1), ("T", 2, 1),
    ("U", 2, 1), ("T", 3, 1), ("U", 3, 1), ("T", 0, 2), ("U", 0, 2), ("T", 1, 2),
    ("U", 1, 2), ("T", 2, 2), ("U", 2, 2), ("T", 3, 2), ("U", 3, 2), ("T", 0, 3),
    ("U", 0, 3), ("T", 1, 3), ("U", 1, 3), ("T", 2, 3), ("U", 2, 3), ("T", 3, 3),
    ("U", 3, 3),
)


def dot(a, b, dims=((1,), (0,)), precision=None):
    return lax.dot_general(
        a, b, (dims, ((), ())), precision=precision, preferred_element_type=F32
    )


def kernel(
    k_hbm, v_hbm, q_hbm, g_hbm, decay_hbm, docs_hbm, gain_hbm, w_hbm, out_hbm,
    rx, pk, docs, gain, pkx, kf, att, abuf, wbuf, st_out, st_in,
    part, longs, shorts, total,
    go, lsem, a2a_s, a2a_r, qg_s, qg_r, pk_s, pk_r, w_s, w_r, wr_s, wr_r, st_sem,
    ag_s, ag_r, l_s, l_r, s_s, s_r, fin_s, fin_r,
):
    c, z, p = lax.axis_index("ctx"), lax.axis_index("head"), lax.axis_index("pipe")
    x, y = lax.rem(c, 4), lax.div(c, 4)

    def at_x(d):
        return 4 * y + lax.rem(x + d, 4)

    def at_y(d):
        return 4 * lax.rem(y + d, 4) + x

    def at_z(d):
        return lax.rem(z + d + 8, 8)

    def block(i, size):
        return pl.ds(pl.multiple_of(i * size, size), size)

    def remote(src, dst, send, recv, dev):
        return pltpu.make_async_remote_copy(
            src_ref=src, dst_ref=dst, send_sem=send, recv_sem=recv,
            device_id=dev, device_id_type=MESH,
        )

    def arrived(dst, recv):
        remote(dst, dst, recv, recv, (c, z, 1 - p)).wait_recv()

    sent = []

    def send(*a):
        copy = remote(*a)
        copy.start()
        sent.append(copy)

    local = [
        pltpu.make_async_copy(src, dst, lsem.at[i])
        for i, (src, dst) in enumerate(
            [
                (ref.at[0, :, block(x, HW)], rx.at[a, x])
                for a, ref in enumerate((k_hbm, v_hbm, q_hbm, g_hbm))
            ]
            + [
                (decay_hbm, pk.at[0:8, :]),
                (docs_hbm, docs),
                (gain_hbm.at[:, block(x, HW)], gain),
                (w_hbm.at[0], wbuf.at[0]),
            ]
        )
    ]
    for i in (4, 5, 6, 0, 1, 2, 3, 7):
        local[i].start()

    yo, half = lax.div(z, 2), lax.rem(z, 2)

    def fin_dev(i):
        return (4 * y + 2 * half + i, 2 * yo + lax.div(x, 2), 1 - p)

    barrier = pltpu.get_barrier_semaphore()
    peers = [(at_x(d), z, p) for d in DELTAS]
    peers += [(at_y(1), z, p), (at_y(3), z, p)]
    peers += [(c, at_z(1), p), (c, at_z(-1), p)]
    peers += [fin_dev(0), fin_dev(1)]
    peers.append((c, z, 1 - p))
    for dev in peers:
        pl.semaphore_signal(barrier, inc=1, device_id=dev, device_id_type=MESH)
    local[4].wait()
    local[5].wait()
    pk[8:16, :] = jnp.broadcast_to(docs[...].astype(F32), (8, TOK))
    pl.semaphore_wait(barrier, len(peers))

    for i, d in enumerate(DELTAS):
        send(pk, pkx.at[x], pk_s.at[i], pk_r.at[i], (at_x(d), z, p))

    def a2a(a, ref):
        for i, d in enumerate(DELTAS):
            to = lax.rem(x + d, 4)
            send(
                ref.at[0, :, block(to, HW)], rx.at[a, x],
                a2a_s.at[a, i], a2a_r.at[a, i], (at_x(d), z, p),
            )

    def a2a_wait(a):
        local[a].wait()
        for i, d in enumerate(DELTAS):
            arrived(rx.at[a, lax.rem(x + 4 - d, 4)], a2a_r.at[a, i])

    def qg_send(j):
        rr = pl.ds(j * CH, CH)
        for a, ref in enumerate((q_hbm, g_hbm)):
            for i, d in enumerate(DELTAS):
                to = lax.rem(x + d, 4)
                remote(
                    ref.at[0, rr, block(to, HW)], rx.at[2 + a, x, rr, :],
                    qg_s.at[a, i, j], qg_r.at[a, i, j], (at_x(d), z, p),
                ).start()

    def qg_wait(a, j):
        for i, d in enumerate(DELTAS):
            src = lax.rem(x + 4 - d, 4)
            arrived(rx.at[2 + a, src, pl.ds(j * CH, CH), :], qg_r.at[a, i, j])

    def w_copy(side, ch):
        rows = pl.ds(ch * HW, HW)
        return remote(
            w_hbm.at[0, rows, :], wbuf.at[(3, 1)[side], rows, :],
            w_s.at[side, ch], w_r.at[side, ch], (at_y((1, 3)[side]), z, p),
        )

    def w_wait(side, ch):
        arrived(wbuf.at[(3, 1)[side], pl.ds(ch * HW, HW), :], w_r.at[side, ch])

    def w_relay_copy(side, ch):
        rows = pl.ds(ch * HW, HW)
        return remote(
            wbuf.at[(3, 1)[side], rows, :], wbuf.at[2, rows, :],
            wr_s.at[ch], wr_r.at[ch], (at_y((1, 3)[side]), z, p),
        )

    def weights(core, chunks):
        @pl.when(p == core)
        def _():
            for side, ch in chunks:
                w_copy(side, ch).start()

    def relays(core):
        @pl.when(p == core)
        def _():
            for ch in range(2):
                for side, i in ((0, ch), (1, 2 + ch)):
                    w_wait(side, i)
                    w_relay_copy(side, i).start()

    @pl.when(p == 0)
    def _():
        pl.semaphore_wait(go, 1)

    a2a(0, k_hbm)
    a2a(1, v_hbm)
    weights(1, ((0, 0), (1, 2), (0, 1), (1, 3)))
    for j in range(3):
        qg_send(j)

    @pl.when(p == 1)
    def _():
        qg_send(3)

    weights(1, ((1, 0), (0, 2), (1, 1)))

    i8 = lax.broadcasted_iota(jnp.int32, (8, 8), 0)
    j8 = lax.broadcasted_iota(jnp.int32, (8, 8), 1)
    pick = (j8 == 2 * x + i8).astype(F32)
    ia = lax.broadcasted_iota(jnp.int32, (TOK, TOK), 0)
    ib = lax.broadcasted_iota(jnp.int32, (TOK, TOK), 1)
    upper = (ia <= ib).astype(F32)
    lower = (ia >= ib).astype(F32)
    eye = (ia == ib).astype(F32)
    for i, d in enumerate(DELTAS):
        arrived(pkx.at[lax.rem(x + 4 - d, 4)], pk_r.at[i])
    pkx[x] = pk[...]
    rows_, cols_, segr, segc = [], [], [], []
    off_r, off_c = jnp.zeros((8, 1), F32), jnp.zeros((1, 8), F32)
    for b in range(4):
        two = dot(pick, pkx[b, 0:8, :], precision=HIGHEST)
        r = dot(two, upper, precision=HIGHEST) + off_r
        s = dot(lower, two, ((1,), (1,)), precision=HIGHEST) + off_c
        e = dot(eye, pkx[b, 8:16, :], ((1,), (1,)), precision=HIGHEST)
        off_r, off_c = r[:, TOK - 1 : TOK], s[TOK - 1 : TOK, :]
        rows_.append(r)
        cols_.append(s)
        segr.append(pkx[b, 8:9, :])
        segc.append(e[:, 0:1])
    last_doc = segr[3][:, TOK - 1 : TOK]

    weights(0, ((1, 2), (1, 3)))
    a2a_wait(0)
    a2a_wait(1)

    @pl.when(p == 1)
    def _():
        pl.semaphore_signal(go, inc=1, device_id=(c, z, 0), device_id_type=MESH)

    for b in range(4):
        keep = (segc[b] == last_doc).astype(F32)
        for h in range(2):
            hs = slice(h, h + 1)
            hh = slice(h * DH, (h + 1) * DH)
            fade = jnp.exp(jnp.minimum(off_c[:, hs] - cols_[b][:, hs], 0.0)) * keep
            kf[b * TOK : (b + 1) * TOK, hh] = (rx[0, b, :, hh].astype(F32) * fade).astype(BF16)
    for h in range(2):
        hh = slice(h * DH, (h + 1) * DH)
        values = rx[1, :, :, hh].reshape(4 * TOK, DH)
        st_out[hh, :] = dot(kf[:, hh], values, ((0,), (0,))).astype(BF16)
    st_out[256:272, :] = jnp.broadcast_to(last_doc, (16, DH)).astype(BF16)
    send(st_out, st_in, st_sem.at[0], st_sem.at[1], (at_y(1), z, p))
    weights(1, ((0, 3),))
    relays(1)
    weights(0, ((0, 0), (0, 1), (0, 2), (1, 0), (0, 3), (1, 1)))

    base = lax.broadcasted_iota(jnp.int32, (TOK, 4 * TOK), 0)
    base = lax.shift_right_logical(base, 5) * TOK + (base & (CH - 1))
    ahead = lax.broadcasted_iota(jnp.int32, (TOK, 4 * TOK), 1) - base
    seg_row = jnp.concatenate(segr, axis=1)
    crow = [jnp.concatenate([r[h : h + 1, :] for r in rows_], axis=1) for h in range(2)]
    later = (y > 0).astype(F32)

    def inside(j):
        rr = slice(j * CH, (j + 1) * CH)
        seg_t = jnp.concatenate([e[rr, :] for e in segc], axis=0)
        allowed = (ahead <= j * CH) & (seg_t == seg_row)
        for h in range(2):
            hh = slice(h * DH, (h + 1) * DH)
            ccol = jnp.concatenate([s[rr, h : h + 1] for s in cols_], axis=0)
            weight = jnp.where(allowed, jnp.exp(jnp.minimum(ccol - crow[h], 0.0)), 0.0)
            queries = rx[2, :, rr, hh].reshape(TOK, DH)
            scores = dot(queries, rx[0, :, :, hh].reshape(4 * TOK, DH), ((1,), (1,)))
            mixed = (scores * weight).astype(BF16)
            att[j, :, hh] = dot(mixed, rx[1, :, :, hh].reshape(4 * TOK, DH))

    def finish(j):
        rr = slice(j * CH, (j + 1) * CH)
        prev_doc = st_in[256:257, 0:1].astype(F32)
        seg_t = jnp.concatenate([e[rr, :] for e in segc], axis=0)
        same = (seg_t == prev_doc).astype(F32) * later
        for h in range(2):
            hh = slice(h * DH, (h + 1) * DH)
            ccol = jnp.concatenate([s[rr, h : h + 1] for s in cols_], axis=0)
            queries = rx[2, :, rr, hh].reshape(TOK, DH)
            full = att[j, :, hh] + dot(queries, st_in[hh, :]) * (jnp.exp(ccol) * same)
            scale = lax.rsqrt(jnp.mean(full * full, axis=-1, keepdims=True) + 1e-06)
            gates = rx[3, :, rr, hh].reshape(TOK, DH).astype(F32)
            normed = full * scale * gain[:, hh] * (1.0 / (1.0 + jnp.exp(-gates)))
            abuf[0, :, rr, hh] = normed.astype(BF16).reshape(4, CH, DH)
        for i, d in enumerate(DELTAS):
            rr = pl.ds(j * CH, CH)
            send(
                abuf.at[0, :, rr, :], abuf.at[1 + i, :, rr, :],
                ag_s.at[i, j], ag_r.at[i, j], (at_x(d), z, p),
            )

    local[2].wait()
    local[3].wait()
    local[6].wait()
    for j in range(4):
        qg_wait(0, j)
        inside(j)
        qg_wait(1, j)
        if j == 0:
            arrived(st_in, st_sem.at[1])
        finish(j)
        if j == 0:

            @pl.when(p == 0)
            def _():
                qg_send(3)

        if j == 2:
            relays(0)
    xs = [lax.rem(x + d, 4) for d in (0, 3, 1, 2)]
    local[7].wait()

    def project(j):
        for i in range(3):
            arrived(abuf.at[1 + i, :, pl.ds(j * CH, CH), :], ag_r.at[i, j])
        if j == 0:
            for ch in range(2):
                w_wait(0, 2 + ch)
                w_wait(1, ch)

        def body(n, carry):
            d = n + lax.div(n, 2)
            acc = jnp.zeros((4 * CH, NW), F32)
            for s in range(4):
                lhs = abuf[s, :, j * CH : (j + 1) * CH, :].reshape(4 * CH, HW)
                acc = acc + dot(lhs, wbuf[d, block(xs[s], HW), :])
            acc = acc.astype(BF16)
            yy = lax.rem(y + d, 4)
            part[j, 2 * yy] = acc[:SH, :]
            part[j, 2 * yy + 1] = acc[SH:, :]
            return carry

        lax.fori_loop(0, 3, body, 0)

    def project_late():
        for ch in range(4):
            arrived(wbuf.at[2, pl.ds(ch * HW, HW), :], wr_r.at[ch])
        yy = lax.rem(y + 2, 4)

        def body(n, carry):
            for i in range(2):
                acc = jnp.zeros((TOK, NW), F32)
                for s in range(4):
                    acc = acc + dot(abuf[s, 2 * n + i], wbuf[2, block(xs[s], HW), :])
                acc = acc.astype(BF16)
                for j in range(4):
                    part[j, 2 * yy + n, i * CH : (i + 1) * CH, :] = acc[j * CH : (j + 1) * CH, :]
            return carry

        lax.fori_loop(0, 2, body, 0)

    def owner(k):
        return lax.rem(z + k + 16, 8)

    def is_late(o):
        return lax.rem(lax.div(o, 2) - y + 4, 4) == 2

    def when(o, late):
        return pl.when(is_late(o) if late else jnp.logical_not(is_late(o)))

    def sign(j):
        return (1, -1)[j % 2]

    def long_copy(src, j, t):
        return remote(
            src, longs.at[j, t], l_s.at[j, t], l_r.at[j, t], (c, at_z(-sign(j)), p)
        )

    def short_copy(src, j, t):
        return remote(
            src, shorts.at[j, t], s_s.at[j, t], s_r.at[j, t], (c, at_z(sign(j)), p)
        )

    def start(j, late):
        s = sign(j)
        lo, so = owner(-4 * s), owner(3 * s)

        @when(lo, late)
        def _():
            long_copy(part.at[j, lo], j, 0).start()

        @when(so, late)
        def _():
            short_copy(part.at[j, so], j, 0).start()

    def fin_copy(j, i):
        return remote(
            total.at[j, pl.ds(i * CH, CH), :],
            out_hbm.at[0, pl.ds(j * CH, CH), block(lax.rem(x, 2), NW)],
            fin_s.at[j, i], fin_r.at[j, lax.rem(x, 2)], fin_dev(i),
        )

    def step(j, t, late):
        s = sign(j)
        lo, so = owner(-s * (3 - t)), owner(s * (2 - t))

        @when(lo, late)
        def _():
            arrived(longs.at[j, t], l_r.at[j, t])
            mine = longs[j, t].astype(F32) + part[j, lo].astype(F32)
            if t < 3:
                longs[j, t] = mine.astype(BF16)
                long_copy(longs.at[j, t], j, t + 1).start()
            else:
                arrived(shorts.at[j, 2], s_r.at[j, 2])
                total[j] = (mine + shorts[j, 2].astype(F32)).astype(BF16)
                for i in range(2):
                    fin_copy(j, i).start()

        if t < 2:

            @when(so, late)
            def _():
                arrived(shorts.at[j, t], s_r.at[j, t])
                mine = shorts[j, t].astype(F32) + part[j, so].astype(F32)
                shorts[j, t] = mine.astype(BF16)
                short_copy(shorts.at[j, t], j, t + 1).start()

    for op in ORDER:
        if op[0] == "S":
            project(op[1])
            start(op[1], False)
        elif op[0] == "L":
            project_late()
            for j in range(4):
                start(j, True)
        else:
            step(op[1], op[2], op[0] == "U")

    for j in range(4):
        for xx in range(2):
            arrived(
                out_hbm.at[0, pl.ds(j * CH, CH), pl.ds(xx * NW, NW)], fin_r.at[j, xx]
            )
        for t in range(4):
            long_copy(longs.at[j, t], j, t).wait_send()
        for t in range(3):
            short_copy(shorts.at[j, t], j, t).wait_send()
        for i in range(2):
            fin_copy(j, i).wait_send()
    for ch in range(4):
        for side in range(2):
            w_copy(side, ch).wait_send()
        w_relay_copy((0, 0, 1, 1)[ch], ch).wait_send()
    for j in range(4):
        for i in range(3):
            for a in range(2):
                rr = rx.at[2 + a, x, pl.ds(j * CH, CH), :]
                remote(rr, rr, qg_s.at[a, i, j], qg_r.at[a, i, j], (c, z, 1 - p)).wait_send()
    for copy in sent:
        copy.wait_send()


def on_device(queries, keys, values, gates, log_decay, segment_ids, norm_gain, out_weight):
    hbm = pl.BlockSpec(memory_space=pltpu.HBM)
    vmem = pltpu.VMEM
    dma = pltpu.SemaphoreType.DMA
    return pl.pallas_call(
        kernel,
        out_shape=jax.ShapeDtypeStruct((1, TOK, 2 * NW), BF16),
        in_specs=[hbm] * 8,
        out_specs=hbm,
        scratch_shapes=[
            vmem((4, 4, TOK, HW), BF16),
            vmem((16, TOK), F32),
            vmem((1, TOK), jnp.int32),
            vmem((1, HW), F32),
            vmem((4, 16, TOK), F32),
            vmem((4 * TOK, HW), BF16),
            vmem((4, TOK, HW), F32),
            vmem((4, 4, TOK, HW), BF16),
            vmem((4, KD, NW), BF16),
            vmem((272, DH), BF16),
            vmem((272, DH), BF16),
            vmem((4, 8, SH, NW), BF16),
            vmem((4, 4, SH, NW), BF16),
            vmem((4, 3, SH, NW), BF16),
            vmem((4, SH, NW), BF16),
            pltpu.SemaphoreType.REGULAR, dma((8,)), dma((2, 3)), dma((2, 3)), dma((2, 3, 4)), dma((2, 3, 4)),
            dma((3,)), dma((3,)),
            dma((2, 4)), dma((2, 4)), dma((4,)), dma((4,)), dma((2,)),
            dma((3, 4)), dma((3, 4)),
            dma((4, 4)), dma((4, 4)), dma((4, 3)), dma((4, 3)),
            dma((4, 2)), dma((4, 2)),
        ],
        compiler_params=pltpu.CompilerParams(
            collective_id=0, has_side_effects=True, vmem_limit_bytes=60 * 2**20
        ),
        cost_estimate=pl.CostEstimate(
            flops=2 * 10**9, bytes_accessed=3 * 2**20, transcendentals=10**6
        ),
    )(
        keys, values, queries, gates, log_decay[0].T, segment_ids, norm_gain, out_weight
    )


def solution(mesh):
    return jax.shard_map(
        on_device,
        mesh=mesh,
        in_specs=(
            P("pipe", "ctx", "head"),
            P("pipe", "ctx", "head"),
            P("pipe", "ctx", "head"),
            P("pipe", "ctx", "head"),
            P("pipe", "ctx", "head"),
            P("pipe", "ctx"),
            P("pipe", "head"),
            P("pipe", "head", "ctx"),
        ),
        out_specs=P("pipe", "ctx", "head"),
        check_vma=False,
    )
```

```python
import jax
import jax.numpy as jnp
from jax import lax
from jax.experimental import pallas as pl
from jax.experimental.pallas import tpu as pltpu
from jax.sharding import PartitionSpec as P

MESH = pl.DeviceIdType.MESH
F32 = jnp.float32
BF16 = jnp.bfloat16
HIGHEST = lax.Precision.HIGHEST

DH = 128
TOK = 128
HW = 256
KD = 1024
NW = 384
CH = 32
SH = 64
DELTAS = (1, 3, 2)
ORDER = (
    ("S", 0), ("S", 1), ("S", 2), ("S", 3), ("L",), ("T", 0, 0),
    ("U", 0, 0), ("T", 1, 0), ("U", 1, 0), ("T", 2, 0), ("U", 2, 0), ("T", 3, 0),
    ("U", 3, 0), ("T", 0, 1), ("U", 0, 1), ("T", 1, 1), ("U", 1, 1), ("T", 2, 1),
    ("U", 2, 1), ("T", 3, 1), ("U", 3, 1), ("T", 0, 2), ("U", 0, 2), ("T", 1, 2),
    ("U", 1, 2), ("T", 2, 2), ("U", 2, 2), ("T", 3, 2), ("U", 3, 2), ("T", 0, 3),
    ("U", 0, 3), ("T", 1, 3), ("U", 1, 3), ("T", 2, 3), ("U", 2, 3), ("T", 3, 3),
    ("U", 3, 3),
)


def dot(a, b, dims=((1,), (0,)), precision=None):
    return lax.dot_general(
        a, b, (dims, ((), ())), precision=precision, preferred_element_type=F32
    )


def kernel(
    k_hbm, v_hbm, q_hbm, g_hbm, decay_hbm, docs_hbm, gain_hbm, w_hbm, out_hbm,
    rx, pk, docs, gain, pkx, kf, att, abuf, wbuf, st_out, st_in,
    part, longs, shorts, total,
    go, lsem, a2a_s, a2a_r, pk_s, pk_r, w_s, w_r, wr_s, wr_r, st_sem,
    ag_s, ag_r, l_s, l_r, s_s, s_r, fin_s, fin_r,
):
    c, z, p = lax.axis_index("ctx"), lax.axis_index("head"), lax.axis_index("pipe")
    x, y = lax.rem(c, 4), lax.div(c, 4)

    def at_x(d):
        return 4 * y + lax.rem(x + d, 4)

    def at_y(d):
        return 4 * lax.rem(y + d, 4) + x

    def at_z(d):
        return lax.rem(z + d + 8, 8)

    def block(i, size):
        return pl.ds(pl.multiple_of(i * size, size), size)

    def remote(src, dst, send, recv, dev):
        return pltpu.make_async_remote_copy(
            src_ref=src, dst_ref=dst, send_sem=send, recv_sem=recv,
            device_id=dev, device_id_type=MESH,
        )

    def arrived(dst, recv):
        remote(dst, dst, recv, recv, (c, z, 1 - p)).wait_recv()

    def send(*a):
        remote(*a).start()

    def all_sent(ref, sem):
        remote(ref, ref, sem, sem, (c, z, 1 - p)).wait_send()

    local = [
        pltpu.make_async_copy(src, dst, lsem.at[i])
        for i, (src, dst) in enumerate(
            [
                (ref.at[0, :, block(x, HW)], rx.at[a, x])
                for a, ref in enumerate((k_hbm, v_hbm, q_hbm, g_hbm))
            ]
            + [
                (decay_hbm, pk.at[0:8, :]),
                (docs_hbm, docs),
                (gain_hbm.at[:, block(x, HW)], gain),
                (w_hbm.at[0], wbuf.at[0]),
            ]
        )
    ]
    for i in (4, 5, 6, 0, 1, 2, 3, 7):
        local[i].start()

    yo, half = lax.div(z, 2), lax.rem(z, 2)

    def fin_dev(i):
        return (4 * y + 2 * half + i, 2 * yo + lax.div(x, 2), 1 - p)

    barrier = pltpu.get_barrier_semaphore()
    peers = [(at_x(d), z, p) for d in DELTAS]
    peers += [(at_y(1), z, p), (at_y(3), z, p)]
    peers += [(c, at_z(1), p), (c, at_z(-1), p)]
    peers += [fin_dev(0), fin_dev(1)]
    peers.append((c, z, 1 - p))
    for dev in peers:
        pl.semaphore_signal(barrier, inc=1, device_id=dev, device_id_type=MESH)
    local[4].wait()
    local[5].wait()
    pk[8:16, :] = jnp.broadcast_to(docs[...].astype(F32), (8, TOK))
    pl.semaphore_wait(barrier, len(peers))

    for i, d in enumerate(DELTAS):
        send(pk, pkx.at[x], pk_s, pk_r, (at_x(d), z, p))

    def a2a(a, ref):
        for i, d in enumerate(DELTAS):
            to = lax.rem(x + d, 4)
            send(
                ref.at[0, :, block(to, HW)], rx.at[a, x],
                a2a_s, a2a_r.at[a], (at_x(d), z, p),
            )

    def a2a_wait(a):
        local[a].wait()
        arrived(rx.at[a, 0:3], a2a_r.at[a])

    def w_copy(side, ch):
        rows = pl.ds(ch * HW, HW)
        first = (ch < 2) == (side == 0)
        return remote(
            w_hbm.at[0, rows, :], wbuf.at[(3, 1)[side], rows, :],
            w_s, w_r.at[ch if first else 4], (at_y((1, 3)[side]), z, p),
        )

    def w_relay_copy(side, ch):
        rows = pl.ds(ch * HW, HW)
        return remote(
            wbuf.at[(3, 1)[side], rows, :], wbuf.at[2, rows, :],
            wr_s, wr_r, (at_y((1, 3)[side]), z, p),
        )

    def weights(core, chunks):
        @pl.when(p == core)
        def _():
            for side, ch in chunks:
                w_copy(side, ch).start()

    def relays(core):
        @pl.when(p == core)
        def _():
            for ch in range(2):
                for side, i in ((0, ch), (1, 2 + ch)):
                    arrived(wbuf.at[(3, 1)[side], pl.ds(i * HW, HW), :], w_r.at[i])
                    w_relay_copy(side, i).start()

    @pl.when(p == 0)
    def _():
        pl.semaphore_wait(go, 1)

    a2a(0, k_hbm)
    a2a(1, v_hbm)
    weights(1, ((0, 0), (1, 2), (0, 1), (1, 3)))
    a2a(2, q_hbm)
    a2a(3, g_hbm)
    weights(1, ((1, 0), (0, 2), (1, 1)))

    i8 = lax.broadcasted_iota(jnp.int32, (8, 8), 0)
    j8 = lax.broadcasted_iota(jnp.int32, (8, 8), 1)
    pick = (j8 == 2 * x + i8).astype(F32)
    ia = lax.broadcasted_iota(jnp.int32, (TOK, TOK), 0)
    ib = lax.broadcasted_iota(jnp.int32, (TOK, TOK), 1)
    upper = (ia <= ib).astype(F32)
    lower = (ia >= ib).astype(F32)
    eye = (ia == ib).astype(F32)
    arrived(pkx.at[0:3], pk_r)
    pkx[x] = pk[...]
    rows_, cols_, segr, segc = [], [], [], []
    off_r, off_c = jnp.zeros((8, 1), F32), jnp.zeros((1, 8), F32)
    for b in range(4):
        two = dot(pick, pkx[b, 0:8, :], precision=HIGHEST)
        r = dot(two, upper, precision=HIGHEST) + off_r
        s = dot(lower, two, ((1,), (1,)), precision=HIGHEST) + off_c
        e = dot(eye, pkx[b, 8:16, :], ((1,), (1,)), precision=HIGHEST)
        off_r, off_c = r[:, TOK - 1 : TOK], s[TOK - 1 : TOK, :]
        rows_.append(r)
        cols_.append(s)
        segr.append(pkx[b, 8:9, :])
        segc.append(e[:, 0:1])
    last_doc = segr[3][:, TOK - 1 : TOK]

    weights(0, ((1, 2), (1, 3)))
    a2a_wait(0)
    a2a_wait(1)

    @pl.when(p == 1)
    def _():
        pl.semaphore_signal(go, inc=1, device_id=(c, z, 0), device_id_type=MESH)

    for b in range(4):
        keep = (segc[b] == last_doc).astype(F32)
        for h in range(2):
            hs = slice(h, h + 1)
            hh = slice(h * DH, (h + 1) * DH)
            fade = jnp.exp(jnp.minimum(off_c[:, hs] - cols_[b][:, hs], 0.0)) * keep
            kf[b * TOK : (b + 1) * TOK, hh] = (rx[0, b, :, hh].astype(F32) * fade).astype(BF16)
    for h in range(2):
        hh = slice(h * DH, (h + 1) * DH)
        values = rx[1, :, :, hh].reshape(4 * TOK, DH)
        st_out[hh, :] = dot(kf[:, hh], values, ((0,), (0,))).astype(BF16)
    st_out[256:272, :] = jnp.broadcast_to(last_doc, (16, DH)).astype(BF16)
    send(st_out, st_in, st_sem.at[0], st_sem.at[1], (at_y(1), z, p))
    weights(1, ((0, 3),))
    relays(1)
    weights(0, ((0, 0), (0, 1), (0, 2), (1, 0), (0, 3), (1, 1)))

    base = lax.broadcasted_iota(jnp.int32, (TOK, 4 * TOK), 0)
    base = lax.shift_right_logical(base, 5) * TOK + (base & (CH - 1))
    ahead = lax.broadcasted_iota(jnp.int32, (TOK, 4 * TOK), 1) - base
    seg_row = jnp.concatenate(segr, axis=1)
    crow = [jnp.concatenate([r[h : h + 1, :] for r in rows_], axis=1) for h in range(2)]
    later = (y > 0).astype(F32)

    def inside(j):
        rr = slice(j * CH, (j + 1) * CH)
        seg_t = jnp.concatenate([e[rr, :] for e in segc], axis=0)
        allowed = (ahead <= j * CH) & (seg_t == seg_row)
        for h in range(2):
            hh = slice(h * DH, (h + 1) * DH)
            ccol = jnp.concatenate([s[rr, h : h + 1] for s in cols_], axis=0)
            weight = jnp.where(allowed, jnp.exp(jnp.minimum(ccol - crow[h], 0.0)), 0.0)
            queries = rx[2, :, rr, hh].reshape(TOK, DH)
            scores = dot(queries, rx[0, :, :, hh].reshape(4 * TOK, DH), ((1,), (1,)))
            mixed = (scores * weight).astype(BF16)
            att[j, :, hh] = dot(mixed, rx[1, :, :, hh].reshape(4 * TOK, DH))

    def finish(j):
        rr = slice(j * CH, (j + 1) * CH)
        prev_doc = st_in[256:257, 0:1].astype(F32)
        seg_t = jnp.concatenate([e[rr, :] for e in segc], axis=0)
        same = (seg_t == prev_doc).astype(F32) * later
        for h in range(2):
            hh = slice(h * DH, (h + 1) * DH)
            ccol = jnp.concatenate([s[rr, h : h + 1] for s in cols_], axis=0)
            queries = rx[2, :, rr, hh].reshape(TOK, DH)
            full = att[j, :, hh] + dot(queries, st_in[hh, :]) * (jnp.exp(ccol) * same)
            scale = lax.rsqrt(jnp.mean(full * full, axis=-1, keepdims=True) + 1e-06)
            gates = rx[3, :, rr, hh].reshape(TOK, DH).astype(F32)
            normed = full * scale * gain[:, hh] * (1.0 / (1.0 + jnp.exp(-gates)))
            abuf[0, :, rr, hh] = normed.astype(BF16).reshape(4, CH, DH)
        for i, d in enumerate(DELTAS):
            rr = pl.ds(j * CH, CH)
            send(
                abuf.at[0, :, rr, :], abuf.at[1 + i, :, rr, :],
                ag_s, ag_r.at[j], (at_x(d), z, p),
            )

    a2a_wait(2)
    local[6].wait()
    for j in range(4):
        inside(j)
        if j == 0:
            a2a_wait(3)
            arrived(st_in, st_sem.at[1])
        finish(j)
        if j == 2:
            relays(0)

    xs = [lax.rem(x + d, 4) for d in (0, 3, 1, 2)]
    local[7].wait()

    def project(j):
        arrived(abuf.at[1:4, :, pl.ds(j * CH, CH), :], ag_r.at[j])
        if j == 0:
            arrived(wbuf.at[1], w_r.at[4])

        def body(n, carry):
            d = n + lax.div(n, 2)
            acc = jnp.zeros((4 * CH, NW), F32)
            for s in range(4):
                lhs = abuf[s, :, j * CH : (j + 1) * CH, :].reshape(4 * CH, HW)
                acc = acc + dot(lhs, wbuf[d, block(xs[s], HW), :])
            acc = acc.astype(BF16)
            yy = lax.rem(y + d, 4)
            part[j, 2 * yy] = acc[:SH, :]
            part[j, 2 * yy + 1] = acc[SH:, :]
            return carry

        lax.fori_loop(0, 3, body, 0)

    def project_late():
        arrived(wbuf.at[2], wr_r)
        yy = lax.rem(y + 2, 4)

        def body(n, carry):
            for i in range(2):
                acc = jnp.zeros((TOK, NW), F32)
                for s in range(4):
                    acc = acc + dot(abuf[s, 2 * n + i], wbuf[2, block(xs[s], HW), :])
                acc = acc.astype(BF16)
                for j in range(4):
                    part[j, 2 * yy + n, i * CH : (i + 1) * CH, :] = acc[j * CH : (j + 1) * CH, :]
            return carry

        lax.fori_loop(0, 2, body, 0)

    def owner(k):
        return lax.rem(z + k + 16, 8)

    def is_late(o):
        return lax.rem(lax.div(o, 2) - y + 4, 4) == 2

    def when(o, late):
        return pl.when(is_late(o) if late else jnp.logical_not(is_late(o)))

    def sign(j):
        return (1, -1)[j % 2]

    def long_copy(src, j, t):
        return remote(
            src, longs.at[j, t], l_s, l_r.at[j, t], (c, at_z(-sign(j)), p)
        )

    def short_copy(src, j, t):
        return remote(
            src, shorts.at[j, t], s_s, s_r.at[j, t], (c, at_z(sign(j)), p)
        )

    def start(j, late):
        s = sign(j)
        lo, so = owner(-4 * s), owner(3 * s)

        @when(lo, late)
        def _():
            long_copy(part.at[j, lo], j, 0).start()

        @when(so, late)
        def _():
            short_copy(part.at[j, so], j, 0).start()

    def fin_copy(j, i):
        return remote(
            total.at[j, pl.ds(i * CH, CH), :],
            out_hbm.at[0, pl.ds(j * CH, CH), block(lax.rem(x, 2), NW)],
            fin_s, fin_r, fin_dev(i),
        )

    def step(j, t, late):
        s = sign(j)
        lo, so = owner(-s * (3 - t)), owner(s * (2 - t))

        @when(lo, late)
        def _():
            arrived(longs.at[j, t], l_r.at[j, t])
            mine = longs[j, t].astype(F32) + part[j, lo].astype(F32)
            if t < 3:
                longs[j, t] = mine.astype(BF16)
                long_copy(longs.at[j, t], j, t + 1).start()
            else:
                arrived(shorts.at[j, 2], s_r.at[j, 2])
                total[j] = (mine + shorts[j, 2].astype(F32)).astype(BF16)
                for i in range(2):
                    fin_copy(j, i).start()

        if t < 2:

            @when(so, late)
            def _():
                arrived(shorts.at[j, t], s_r.at[j, t])
                mine = shorts[j, t].astype(F32) + part[j, so].astype(F32)
                shorts[j, t] = mine.astype(BF16)
                short_copy(shorts.at[j, t], j, t + 1).start()

    for op in ORDER:
        if op[0] == "S":
            project(op[1])
            start(op[1], False)
        elif op[0] == "L":
            project_late()
            for j in range(4):
                start(j, True)
        else:
            step(op[1], op[2], op[0] == "U")

    arrived(out_hbm.at[0], fin_r)
    all_sent(pkx.at[0:3], pk_s)
    all_sent(rx.at[0:3], a2a_s)
    all_sent(wbuf.at[0:2], w_s)
    all_sent(wbuf.at[2], wr_s)
    all_sent(st_out, st_sem.at[0])
    all_sent(abuf.at[0:3], ag_s)
    all_sent(longs, l_s)
    all_sent(shorts, s_s)
    all_sent(total, fin_s)


def on_device(queries, keys, values, gates, log_decay, segment_ids, norm_gain, out_weight):
    hbm = pl.BlockSpec(memory_space=pltpu.HBM)
    vmem = pltpu.VMEM
    dma = pltpu.SemaphoreType.DMA
    return pl.pallas_call(
        kernel,
        out_shape=jax.ShapeDtypeStruct((1, TOK, 2 * NW), BF16),
        in_specs=[hbm] * 8,
        out_specs=hbm,
        scratch_shapes=[
            vmem((4, 4, TOK, HW), BF16),
            vmem((16, TOK), F32),
            vmem((1, TOK), jnp.int32),
            vmem((1, HW), F32),
            vmem((4, 16, TOK), F32),
            vmem((4 * TOK, HW), BF16),
            vmem((4, TOK, HW), F32),
            vmem((4, 4, TOK, HW), BF16),
            vmem((4, KD, NW), BF16),
            vmem((272, DH), BF16),
            vmem((272, DH), BF16),
            vmem((4, 8, SH, NW), BF16),
            vmem((4, 4, SH, NW), BF16),
            vmem((4, 3, SH, NW), BF16),
            vmem((4, SH, NW), BF16),
            pltpu.SemaphoreType.REGULAR, dma((8,)), dma, dma((4,)), dma, dma,
            dma, dma((5,)), dma, dma, dma((2,)), dma, dma((4,)),
            dma, dma((4, 4)), dma, dma((4, 3)), dma, dma,
        ],
        compiler_params=pltpu.CompilerParams(
            collective_id=0, has_side_effects=True, vmem_limit_bytes=60 * 2**20
        ),
        cost_estimate=pl.CostEstimate(
            flops=2 * 10**9, bytes_accessed=3 * 2**20, transcendentals=10**6
        ),
    )(
        keys, values, queries, gates, log_decay[0].T, segment_ids, norm_gain, out_weight
    )


def solution(mesh):
    return jax.shard_map(
        on_device,
        mesh=mesh,
        in_specs=(
            P("pipe", "ctx", "head"),
            P("pipe", "ctx", "head"),
            P("pipe", "ctx", "head"),
            P("pipe", "ctx", "head"),
            P("pipe", "ctx", "head"),
            P("pipe", "ctx"),
            P("pipe", "head"),
            P("pipe", "head", "ctx"),
        ),
        out_specs=P("pipe", "ctx", "head"),
        check_vma=False,
    )
```

```python
import jax
import jax.numpy as jnp
from jax import lax
from jax.experimental import pallas as pl
from jax.experimental.pallas import tpu as pltpu
from jax.sharding import PartitionSpec as P

MESH = pl.DeviceIdType.MESH
F32 = jnp.float32
BF16 = jnp.bfloat16
HIGHEST = lax.Precision.HIGHEST

DH = 128
TOK = 128
HW = 256
KD = 1024
NW = 384
CH = 32
SH = 64
DELTAS = (1, 3, 2)

EARLY = ((), ((0, 0),), ((1, 0),), ((2, 0), (0, 1)))


def dot(a, b, dims=((1,), (0,)), precision=None):
    return lax.dot_general(
        a, b, (dims, ((), ())), precision=precision, preferred_element_type=F32
    )


def kernel(
    k_hbm, v_hbm, q_hbm, g_hbm, decay_hbm, docs_hbm, gain_hbm, w_hbm, out_hbm,
    rx, pk, docs, gain, pkx, kf, att, abuf, wbuf, st_out, st_in,
    part, land, total,
    go, lsem, a2a_s, a2a_r, pk_s, pk_r, w_s, w_r, wr_s, wr_r, st_sem,
    ag_s, ag_r, z_s, z_r, fin_s, fin_r,
):
    c, z, p = lax.axis_index("ctx"), lax.axis_index("head"), lax.axis_index("pipe")
    x, y = lax.rem(c, 4), lax.div(c, 4)

    def at_x(d):
        return 4 * y + lax.rem(x + d, 4)

    def at_y(d):
        return 4 * lax.rem(y + d, 4) + x

    def at_z(d):
        return lax.rem(z + d + 8, 8)

    def block(i, size):
        return pl.ds(pl.multiple_of(i * size, size), size)

    def remote(src, dst, send, recv, dev):
        return pltpu.make_async_remote_copy(
            src_ref=src, dst_ref=dst, send_sem=send, recv_sem=recv,
            device_id=dev, device_id_type=MESH,
        )

    def arrived(dst, recv):
        remote(dst, dst, recv, recv, (c, z, 1 - p)).wait_recv()

    def send(*a):
        remote(*a).start()

    def all_sent(ref, sem):
        remote(ref, ref, sem, sem, (c, z, 1 - p)).wait_send()

    local = [
        pltpu.make_async_copy(src, dst, lsem.at[i])
        for i, (src, dst) in enumerate(
            [
                (ref.at[0, :, block(x, HW)], rx.at[a, x])
                for a, ref in enumerate((k_hbm, v_hbm, q_hbm, g_hbm))
            ]
            + [
                (decay_hbm, pk.at[0:8, :]),
                (docs_hbm, docs),
                (gain_hbm.at[:, block(x, HW)], gain),
                (w_hbm.at[0], wbuf.at[0]),
            ]
        )
    ]
    for i in (4, 5, 6, 0, 1, 2, 3, 7):
        local[i].start()

    yo, half = lax.div(z, 2), lax.rem(z, 2)

    def fin_dev(i):
        return (4 * y + 2 * half + i, 2 * yo + lax.div(x, 2), 1 - p)

    barrier = pltpu.get_barrier_semaphore()
    peers = [(at_x(d), z, p) for d in DELTAS]
    peers += [(at_y(1), z, p), (at_y(3), z, p)]
    peers += [(c, at_z(d), p) for d in (1, -1, 2, -2)]
    peers += [fin_dev(0), fin_dev(1)]
    peers.append((c, z, 1 - p))
    for dev in peers:
        pl.semaphore_signal(barrier, inc=1, device_id=dev, device_id_type=MESH)
    local[4].wait()
    local[5].wait()
    pk[8:16, :] = jnp.broadcast_to(docs[...].astype(F32), (8, TOK))
    pl.semaphore_wait(barrier, len(peers))

    for i, d in enumerate(DELTAS):
        send(pk, pkx.at[x], pk_s, pk_r, (at_x(d), z, p))

    def a2a(a, ref):
        for i, d in enumerate(DELTAS):
            to = lax.rem(x + d, 4)
            send(
                ref.at[0, :, block(to, HW)], rx.at[a, x],
                a2a_s, a2a_r.at[a], (at_x(d), z, p),
            )

    def a2a_wait(a):
        local[a].wait()
        arrived(rx.at[a, 0:3], a2a_r.at[a])

    def w_copy(side, ch):
        rows = pl.ds(ch * HW, HW)
        first = (ch < 2) == (side == 0)
        return remote(
            w_hbm.at[0, rows, :], wbuf.at[(3, 1)[side], rows, :],
            w_s, w_r.at[ch if first else 4], (at_y((1, 3)[side]), z, p),
        )

    def w_relay_copy(side, ch):
        rows = pl.ds(ch * HW, HW)
        return remote(
            wbuf.at[(3, 1)[side], rows, :], wbuf.at[2, rows, :],
            wr_s, wr_r, (at_y((1, 3)[side]), z, p),
        )

    def weights(core, chunks):
        @pl.when(p == core)
        def _():
            for side, ch in chunks:
                w_copy(side, ch).start()

    def relays(core):
        @pl.when(p == core)
        def _():
            for ch in range(2):
                for side, i in ((0, ch), (1, 2 + ch)):
                    arrived(wbuf.at[(3, 1)[side], pl.ds(i * HW, HW), :], w_r.at[i])
                    w_relay_copy(side, i).start()

    @pl.when(p == 0)
    def _():
        pl.semaphore_wait(go, 1)

    a2a(0, k_hbm)
    a2a(1, v_hbm)
    weights(1, ((0, 0), (1, 2), (0, 1), (1, 3)))
    a2a(2, q_hbm)
    a2a(3, g_hbm)
    weights(1, ((1, 0), (0, 2), (1, 1)))

    i8 = lax.broadcasted_iota(jnp.int32, (8, 8), 0)
    j8 = lax.broadcasted_iota(jnp.int32, (8, 8), 1)
    pick = (j8 == 2 * x + i8).astype(F32)
    ia = lax.broadcasted_iota(jnp.int32, (TOK, TOK), 0)
    ib = lax.broadcasted_iota(jnp.int32, (TOK, TOK), 1)
    upper = (ia <= ib).astype(F32)
    lower = (ia >= ib).astype(F32)
    eye = (ia == ib).astype(F32)
    arrived(pkx.at[0:3], pk_r)
    pkx[x] = pk[...]
    rows_, cols_, segr, segc = [], [], [], []
    off_r, off_c = jnp.zeros((8, 1), F32), jnp.zeros((1, 8), F32)
    for b in range(4):
        two = dot(pick, pkx[b, 0:8, :], precision=HIGHEST)
        r = dot(two, upper, precision=HIGHEST) + off_r
        s = dot(lower, two, ((1,), (1,)), precision=HIGHEST) + off_c
        e = dot(eye, pkx[b, 8:16, :], ((1,), (1,)), precision=HIGHEST)
        off_r, off_c = r[:, TOK - 1 : TOK], s[TOK - 1 : TOK, :]
        rows_.append(r)
        cols_.append(s)
        segr.append(pkx[b, 8:9, :])
        segc.append(e[:, 0:1])
    last_doc = segr[3][:, TOK - 1 : TOK]

    weights(0, ((1, 2), (1, 3)))
    a2a_wait(0)
    a2a_wait(1)

    @pl.when(p == 1)
    def _():
        pl.semaphore_signal(go, inc=1, device_id=(c, z, 0), device_id_type=MESH)

    for b in range(4):
        keep = (segc[b] == last_doc).astype(F32)
        for h in range(2):
            hs = slice(h, h + 1)
            hh = slice(h * DH, (h + 1) * DH)
            fade = jnp.exp(jnp.minimum(off_c[:, hs] - cols_[b][:, hs], 0.0)) * keep
            kf[b * TOK : (b + 1) * TOK, hh] = (rx[0, b, :, hh].astype(F32) * fade).astype(BF16)
    for h in range(2):
        hh = slice(h * DH, (h + 1) * DH)
        values = rx[1, :, :, hh].reshape(4 * TOK, DH)
        st_out[hh, :] = dot(kf[:, hh], values, ((0,), (0,))).astype(BF16)
    st_out[256:272, :] = jnp.broadcast_to(last_doc, (16, DH)).astype(BF16)
    send(st_out, st_in, st_sem.at[0], st_sem.at[1], (at_y(1), z, p))
    weights(1, ((0, 3),))
    relays(1)
    weights(0, ((0, 0), (0, 1), (0, 2), (1, 0), (0, 3), (1, 1)))

    base = lax.broadcasted_iota(jnp.int32, (TOK, 4 * TOK), 0)
    base = lax.shift_right_logical(base, 5) * TOK + (base & (CH - 1))
    ahead = lax.broadcasted_iota(jnp.int32, (TOK, 4 * TOK), 1) - base
    seg_row = jnp.concatenate(segr, axis=1)
    crow = [jnp.concatenate([r[h : h + 1, :] for r in rows_], axis=1) for h in range(2)]
    later = (y > 0).astype(F32)

    def inside(j):
        rr = slice(j * CH, (j + 1) * CH)
        seg_t = jnp.concatenate([e[rr, :] for e in segc], axis=0)
        allowed = (ahead <= j * CH) & (seg_t == seg_row)
        for h in range(2):
            hh = slice(h * DH, (h + 1) * DH)
            ccol = jnp.concatenate([s[rr, h : h + 1] for s in cols_], axis=0)
            weight = jnp.where(allowed, jnp.exp(jnp.minimum(ccol - crow[h], 0.0)), 0.0)
            queries = rx[2, :, rr, hh].reshape(TOK, DH)
            scores = dot(queries, rx[0, :, :, hh].reshape(4 * TOK, DH), ((1,), (1,)))
            mixed = (scores * weight).astype(BF16)
            att[j, :, hh] = dot(mixed, rx[1, :, :, hh].reshape(4 * TOK, DH))

    def finish(j):
        rr = slice(j * CH, (j + 1) * CH)
        prev_doc = st_in[256:257, 0:1].astype(F32)
        seg_t = jnp.concatenate([e[rr, :] for e in segc], axis=0)
        same = (seg_t == prev_doc).astype(F32) * later
        for h in range(2):
            hh = slice(h * DH, (h + 1) * DH)
            ccol = jnp.concatenate([s[rr, h : h + 1] for s in cols_], axis=0)
            queries = rx[2, :, rr, hh].reshape(TOK, DH)
            full = att[j, :, hh] + dot(queries, st_in[hh, :]) * (jnp.exp(ccol) * same)
            scale = lax.rsqrt(jnp.mean(full * full, axis=-1, keepdims=True) + 1e-06)
            gates = rx[3, :, rr, hh].reshape(TOK, DH).astype(F32)
            normed = full * scale * gain[:, hh] * (1.0 / (1.0 + jnp.exp(-gates)))
            abuf[0, :, rr, hh] = normed.astype(BF16).reshape(4, CH, DH)
        for i, d in enumerate(DELTAS):
            rr = pl.ds(j * CH, CH)
            send(
                abuf.at[0, :, rr, :], abuf.at[1 + i, :, rr, :],
                ag_s, ag_r.at[j], (at_x(d), z, p),
            )

    a2a_wait(2)
    local[6].wait()
    for j in range(4):
        inside(j)
    a2a_wait(3)
    arrived(st_in, st_sem.at[1])
    for j in range(4):
        finish(j)
        if j == 3:
            relays(0)

    xs = [lax.rem(x + d, 4) for d in (0, 3, 1, 2)]
    local[7].wait()

    def project(j):
        arrived(abuf.at[1:4, :, pl.ds(j * CH, CH), :], ag_r.at[j])
        if j == 0:
            arrived(wbuf.at[1], w_r.at[4])

        def body(n, carry):
            d = n + lax.div(n, 2)
            acc = jnp.zeros((4 * CH, NW), F32)
            for s in range(4):
                lhs = abuf[s, :, j * CH : (j + 1) * CH, :].reshape(4 * CH, HW)
                acc = acc + dot(lhs, wbuf[d, block(xs[s], HW), :])
            acc = acc.astype(BF16)
            yy = lax.rem(y + d, 4)
            part[j, 2 * yy] = acc[:SH, :]
            part[j, 2 * yy + 1] = acc[SH:, :]
            return carry

        lax.fori_loop(0, 3, body, 0)

    def project_late():
        arrived(wbuf.at[2], wr_r)
        yy = lax.rem(y + 2, 4)

        def body(n, carry):
            for i in range(2):
                acc = jnp.zeros((TOK, NW), F32)
                for s in range(4):
                    acc = acc + dot(abuf[s, 2 * n + i], wbuf[2, block(xs[s], HW), :])
                acc = acc.astype(BF16)
                for j in range(4):
                    part[j, 2 * yy + n, i * CH : (i + 1) * CH, :] = acc[j * CH : (j + 1) * CH, :]
            return carry

        lax.fori_loop(0, 2, body, 0)

    def owner(k):
        return lax.rem(z + k + 16, 8)

    def is_late(o):
        return lax.rem(lax.div(o, 2) - y + 4, 4) == 2

    def when(o, late):
        return pl.when(is_late(o) if late else jnp.logical_not(is_late(o)))

    def sign(j):
        return (1, -1)[j % 2]

    def z_copy(src, j, slot, d):
        return remote(
            src, land.at[j, slot], z_s, z_r.at[j, slot], (c, at_z(sign(j) * d), p)
        )

    def landed(j, slot):
        arrived(land.at[j, slot], z_r.at[j, slot])
        return land[j, slot].astype(F32)

    def mine(j, o):
        return part[j, o].astype(F32)

    def start(j, late):
        for slot, d, to in ((0, -4, -1), (4, 3, 1)):
            o = owner(sign(j) * d)

            @when(o, late)
            def _():
                z_copy(part.at[j, o], j, slot, to).start()

    def start_short(j, late):
        for slot, d, to in ((0, -4, -2), (1, -3, -1), (2, 3, 1), (3, -1, -1), (4, 1, 1)):
            o = owner(sign(j) * d)

            @when(o, late)
            def _():
                z_copy(part.at[j, o], j, slot, to).start()

    def fin_copy(j, i):
        return remote(
            total.at[j, pl.ds(i * CH, CH), :],
            out_hbm.at[0, pl.ds(j * CH, CH), block(lax.rem(x, 2), NW)],
            fin_s, fin_r, fin_dev(i),
        )

    def finished(j, acc):
        total[j] = acc.astype(BF16)
        for i in range(2):
            fin_copy(j, i).start()

    def step(j, t, late):
        s = sign(j)
        lo, so = owner(-s * (3 - t)), owner(s * (2 - t))

        @when(lo, late)
        def _():
            acc = mine(j, lo) + landed(j, t)
            if t < 3:
                land[j, t] = acc.astype(BF16)
                z_copy(land.at[j, t], j, t + 1, -1).start()
            else:
                finished(j, acc + landed(j, 6))

        if t < 2:

            @when(so, late)
            def _():
                land[j, 4 + t] = (mine(j, so) + landed(j, 4 + t)).astype(BF16)
                z_copy(land.at[j, 4 + t], j, 5 + t, 1).start()

    def middle(j, late):
        lo, so = owner(-2 * sign(j)), owner(2 * sign(j))

        @when(lo, late)
        def _():
            land[j, 0] = (mine(j, lo) + landed(j, 0) + landed(j, 1)).astype(BF16)
            z_copy(land.at[j, 0], j, 5, -2).start()

        @when(so, late)
        def _():
            land[j, 2] = (mine(j, so) + landed(j, 2)).astype(BF16)
            z_copy(land.at[j, 2], j, 6, 2).start()

    def end(j, late):
        @when(owner(0), late)
        def _():
            acc = mine(j, z)
            for slot in (3, 4, 5, 6):
                acc = acc + landed(j, slot)
            finished(j, acc)

    def begin(j, late):
        @pl.when(p == 1)
        def _():
            start(j, late)

        @pl.when(p == 0)
        def _():
            start_short(j, late)

    for j in range(4):
        project(j)
        begin(j, False)

        @pl.when(p == 1)
        def _():
            for i, t in EARLY[j]:
                step(i, t, False)

    project_late()
    for j in range(4):
        begin(j, True)

    @pl.when(p == 1)
    def _():
        for t in range(4):
            for j in range(4):
                if (j, t) not in sum(EARLY, ()):
                    step(j, t, False)
                step(j, t, True)

    @pl.when(p == 0)
    def _():
        for work in (middle, end):
            for j in range(4):
                work(j, False)
                work(j, True)

    arrived(out_hbm.at[0], fin_r)
    all_sent(pkx.at[0:3], pk_s)
    all_sent(rx.at[0:3], a2a_s)
    all_sent(wbuf.at[0:2], w_s)
    all_sent(wbuf.at[2], wr_s)
    all_sent(st_out, st_sem.at[0])
    all_sent(abuf.at[0:3], ag_s)
    all_sent(land, z_s)
    all_sent(total, fin_s)


def on_device(queries, keys, values, gates, log_decay, segment_ids, norm_gain, out_weight):
    hbm = pl.BlockSpec(memory_space=pltpu.HBM)
    vmem = pltpu.VMEM
    dma = pltpu.SemaphoreType.DMA
    return pl.pallas_call(
        kernel,
        out_shape=jax.ShapeDtypeStruct((1, TOK, 2 * NW), BF16),
        in_specs=[hbm] * 8,
        out_specs=hbm,
        scratch_shapes=[
            vmem((4, 4, TOK, HW), BF16),
            vmem((16, TOK), F32),
            vmem((1, TOK), jnp.int32),
            vmem((1, HW), F32),
            vmem((4, 16, TOK), F32),
            vmem((4 * TOK, HW), BF16),
            vmem((4, TOK, HW), F32),
            vmem((4, 4, TOK, HW), BF16),
            vmem((4, KD, NW), BF16),
            vmem((272, DH), BF16),
            vmem((272, DH), BF16),
            vmem((4, 8, SH, NW), BF16),
            vmem((4, 7, SH, NW), BF16),
            vmem((4, SH, NW), BF16),
            pltpu.SemaphoreType.REGULAR, dma((8,)), dma, dma((4,)), dma, dma,
            dma, dma((5,)), dma, dma, dma((2,)), dma, dma((4,)),
            dma, dma((4, 7)), dma, dma,
        ],
        compiler_params=pltpu.CompilerParams(
            collective_id=0, has_side_effects=True, vmem_limit_bytes=60 * 2**20
        ),
        cost_estimate=pl.CostEstimate(
            flops=2 * 10**9, bytes_accessed=3 * 2**20, transcendentals=10**6
        ),
    )(
        keys, values, queries, gates, log_decay[0].T, segment_ids, norm_gain, out_weight
    )


def solution(mesh):
    return jax.shard_map(
        on_device,
        mesh=mesh,
        in_specs=(
            P("pipe", "ctx", "head"),
            P("pipe", "ctx", "head"),
            P("pipe", "ctx", "head"),
            P("pipe", "ctx", "head"),
            P("pipe", "ctx", "head"),
            P("pipe", "ctx"),
            P("pipe", "head"),
            P("pipe", "head", "ctx"),
        ),
        out_specs=P("pipe", "ctx", "head"),
        check_vma=False,
    )
```

```python
import jax
import jax.numpy as jnp
from jax import lax
from jax.experimental import pallas as pl
from jax.experimental.pallas import tpu as pltpu
from jax.sharding import PartitionSpec as P

MESH = pl.DeviceIdType.MESH
F32 = jnp.float32
BF16 = jnp.bfloat16
HIGHEST = lax.Precision.HIGHEST

DH = 128
TOK = 128
HW = 256
KD = 1024
NW = 384
CH = 32
SH = 64
DELTAS = (1, 3, 2)
ORDER = (
    ("S", 0), ("S", 1), ("S", 2), ("S", 3), ("L",), ("T", 0, 0),
    ("U", 0, 0), ("T", 1, 0), ("U", 1, 0), ("T", 2, 0), ("U", 2, 0), ("T", 3, 0),
    ("U", 3, 0), ("T", 0, 1), ("U", 0, 1), ("T", 1, 1), ("U", 1, 1), ("T", 2, 1),
    ("U", 2, 1), ("T", 3, 1), ("U", 3, 1), ("T", 0, 2), ("U", 0, 2), ("T", 1, 2),
    ("U", 1, 2), ("T", 2, 2), ("U", 2, 2), ("T", 3, 2), ("U", 3, 2), ("T", 0, 3),
    ("U", 0, 3), ("T", 1, 3), ("U", 1, 3), ("T", 2, 3), ("U", 2, 3), ("T", 3, 3),
    ("U", 3, 3),
)


def dot(a, b, dims=((1,), (0,)), precision=None):
    return lax.dot_general(
        a, b, (dims, ((), ())), precision=precision, preferred_element_type=F32
    )


def kernel(
    k_hbm, v_hbm, q_hbm, g_hbm, decay_hbm, docs_hbm, gain_hbm, w_hbm, out_hbm,
    rx, pk, docs, gain, pkx, kf, att, abuf, wbuf, st_out, st_in,
    part, longs, shorts, total,
    go, lsem, a2a_s, a2a_r, pk_s, pk_r, w_s, w_r, wr_s, wr_r, st_sem,
    ag_s, ag_r, l_s, l_r, s_s, s_r, fin_s, fin_r,
):
    c, z, p = lax.axis_index("ctx"), lax.axis_index("head"), lax.axis_index("pipe")
    x, y = lax.rem(c, 4), lax.div(c, 4)

    def at_x(d):
        return 4 * y + lax.rem(x + d, 4)

    def at_y(d):
        return 4 * lax.rem(y + d, 4) + x

    def at_z(d):
        return lax.rem(z + d + 8, 8)

    def block(i, size):
        return pl.ds(pl.multiple_of(i * size, size), size)

    def remote(src, dst, send, recv, dev):
        return pltpu.make_async_remote_copy(
            src_ref=src, dst_ref=dst, send_sem=send, recv_sem=recv,
            device_id=dev, device_id_type=MESH,
        )

    def arrived(dst, recv):
        remote(dst, dst, recv, recv, (c, z, 1 - p)).wait_recv()

    def send(*a):
        remote(*a).start()

    def all_sent(ref, sem):
        remote(ref, ref, sem, sem, (c, z, 1 - p)).wait_send()

    local = [
        pltpu.make_async_copy(src, dst, a2a_r.at[i] if i < 4 else lsem.at[i - 4])
        for i, (src, dst) in enumerate(
            [
                (ref.at[0, :, block(x, HW)], rx.at[a, x])
                for a, ref in enumerate((k_hbm, v_hbm, q_hbm, g_hbm))
            ]
            + [
                (decay_hbm, pk.at[0:8, :]),
                (docs_hbm, docs),
                (gain_hbm.at[:, block(x, HW)], gain),
                (w_hbm.at[0], wbuf.at[0]),
            ]
        )
    ]
    for i in (4, 5, 6, 0, 1, 2, 3, 7):
        local[i].start()

    yo, half = lax.div(z, 2), lax.rem(z, 2)

    def fin_dev(i):
        return (4 * y + 2 * half + i, 2 * yo + lax.div(x, 2), 1 - p)

    barrier = pltpu.get_barrier_semaphore()
    peers = [(at_x(d), z, p) for d in DELTAS]
    peers += [(at_y(1), z, p), (at_y(3), z, p)]
    peers += [(c, at_z(1), p), (c, at_z(-1), p)]
    peers += [fin_dev(0), fin_dev(1)]
    peers.append((c, z, 1 - p))
    for dev in peers:
        pl.semaphore_signal(barrier, inc=1, device_id=dev, device_id_type=MESH)
    local[4].wait()
    local[5].wait()
    pk[8:16, :] = jnp.broadcast_to(docs[...].astype(F32), (8, TOK))
    pl.semaphore_wait(barrier, len(peers))

    for i, d in enumerate(DELTAS):
        send(pk, pkx.at[x], pk_s, pk_r, (at_x(d), z, p))

    def a2a(a, ref):
        for i, d in enumerate(DELTAS):
            to = lax.rem(x + d, 4)
            send(
                ref.at[0, :, block(to, HW)], rx.at[a, x],
                a2a_s, a2a_r.at[a], (at_x(d), z, p),
            )

    def a2a_wait(a):
        arrived(rx.at[a], a2a_r.at[a])

    def w_copy(side, ch):
        rows = pl.ds(ch * HW, HW)
        first = (ch < 2) == (side == 0)
        return remote(
            w_hbm.at[0, rows, :], wbuf.at[(3, 1)[side], rows, :],
            w_s, w_r.at[ch if first else 4], (at_y((1, 3)[side]), z, p),
        )

    def w_relay_copy(side, ch):
        rows = pl.ds(ch * HW, HW)
        return remote(
            wbuf.at[(3, 1)[side], rows, :], wbuf.at[2, rows, :],
            wr_s, wr_r, (at_y((1, 3)[side]), z, p),
        )

    def weights(core, chunks):
        @pl.when(p == core)
        def _():
            for side, ch in chunks:
                w_copy(side, ch).start()

    def relays(core):
        @pl.when(p == core)
        def _():
            for ch in range(2):
                for side, i in ((0, ch), (1, 2 + ch)):
                    arrived(wbuf.at[(3, 1)[side], pl.ds(i * HW, HW), :], w_r.at[i])
                    w_relay_copy(side, i).start()

    @pl.when(p == 0)
    def _():
        pl.semaphore_wait(go, 1)

    a2a(0, k_hbm)
    a2a(1, v_hbm)
    weights(1, ((0, 0), (1, 2), (0, 1), (1, 3)))
    @pl.when(p == 1)
    def _():
        a2a(2, q_hbm)
        a2a(3, g_hbm)

    weights(1, ((1, 0), (0, 2), (1, 1)))

    i8 = lax.broadcasted_iota(jnp.int32, (8, 8), 0)
    j8 = lax.broadcasted_iota(jnp.int32, (8, 8), 1)
    pick = (j8 == 2 * x + i8).astype(F32)
    ia = lax.broadcasted_iota(jnp.int32, (TOK, TOK), 0)
    ib = lax.broadcasted_iota(jnp.int32, (TOK, TOK), 1)
    upper = (ia <= ib).astype(F32)
    lower = (ia >= ib).astype(F32)
    eye = (ia == ib).astype(F32)
    arrived(pkx.at[0:3], pk_r)
    pkx[x] = pk[...]
    rows_, cols_, segr, segc = [], [], [], []
    off_r, off_c = jnp.zeros((8, 1), F32), jnp.zeros((1, 8), F32)
    for b in range(4):
        two = dot(pick, pkx[b, 0:8, :], precision=HIGHEST)
        r = dot(two, upper, precision=HIGHEST) + off_r
        s = dot(lower, two, ((1,), (1,)), precision=HIGHEST) + off_c
        e = dot(eye, pkx[b, 8:16, :], ((1,), (1,)), precision=HIGHEST)
        off_r, off_c = r[:, TOK - 1 : TOK], s[TOK - 1 : TOK, :]
        rows_.append(r)
        cols_.append(s)
        segr.append(pkx[b, 8:9, :])
        segc.append(e[:, 0:1])
    last_doc = segr[3][:, TOK - 1 : TOK]

    @pl.when(p == 0)
    def _():
        a2a(2, q_hbm)
        a2a(3, g_hbm)

    weights(0, ((1, 2), (1, 3)))
    a2a_wait(0)
    a2a_wait(1)

    @pl.when(p == 1)
    def _():
        pl.semaphore_signal(go, inc=1, device_id=(c, z, 0), device_id_type=MESH)

    for b in range(4):
        keep = (segc[b] == last_doc).astype(F32)
        for h in range(2):
            hs = slice(h, h + 1)
            hh = slice(h * DH, (h + 1) * DH)
            fade = jnp.exp(jnp.minimum(off_c[:, hs] - cols_[b][:, hs], 0.0)) * keep
            kf[b * TOK : (b + 1) * TOK, hh] = (rx[0, b, :, hh].astype(F32) * fade).astype(BF16)
    for h in range(2):
        hh = slice(h * DH, (h + 1) * DH)
        values = rx[1, :, :, hh].reshape(4 * TOK, DH)
        st_out[hh, :] = dot(kf[:, hh], values, ((0,), (0,))).astype(BF16)
    st_out[256:272, :] = jnp.broadcast_to(last_doc, (16, DH)).astype(BF16)
    send(st_out, st_in, st_sem.at[0], st_sem.at[1], (at_y(1), z, p))
    weights(1, ((0, 3),))
    relays(1)
    weights(0, ((0, 0), (0, 1), (0, 2), (1, 0), (0, 3), (1, 1)))

    base = lax.broadcasted_iota(jnp.int32, (TOK, 4 * TOK), 0)
    base = lax.shift_right_logical(base, 5) * TOK + (base & (CH - 1))
    ahead = lax.broadcasted_iota(jnp.int32, (TOK, 4 * TOK), 1) - base
    seg_row = jnp.concatenate(segr, axis=1)
    crow = [jnp.concatenate([r[h : h + 1, :] for r in rows_], axis=1) for h in range(2)]
    later = (y > 0).astype(F32)

    def inside(j):
        rr = slice(j * CH, (j + 1) * CH)
        seg_t = jnp.concatenate([e[rr, :] for e in segc], axis=0)
        allowed = (ahead <= j * CH) & (seg_t == seg_row)
        for h in range(2):
            hh = slice(h * DH, (h + 1) * DH)
            ccol = jnp.concatenate([s[rr, h : h + 1] for s in cols_], axis=0)
            weight = jnp.where(allowed, jnp.exp(jnp.minimum(ccol - crow[h], 0.0)), 0.0)
            queries = rx[2, :, rr, hh].reshape(TOK, DH)
            scores = dot(queries, rx[0, :, :, hh].reshape(4 * TOK, DH), ((1,), (1,)))
            mixed = (scores * weight).astype(BF16)
            att[j, :, hh] = dot(mixed, rx[1, :, :, hh].reshape(4 * TOK, DH))

    def finish(j):
        rr = slice(j * CH, (j + 1) * CH)
        prev_doc = st_in[256:257, 0:1].astype(F32)
        seg_t = jnp.concatenate([e[rr, :] for e in segc], axis=0)
        same = (seg_t == prev_doc).astype(F32) * later
        for h in range(2):
            hh = slice(h * DH, (h + 1) * DH)
            ccol = jnp.concatenate([s[rr, h : h + 1] for s in cols_], axis=0)
            queries = rx[2, :, rr, hh].reshape(TOK, DH)
            full = att[j, :, hh] + dot(queries, st_in[hh, :]) * (jnp.exp(ccol) * same)
            scale = lax.rsqrt(jnp.mean(full * full, axis=-1, keepdims=True) + 1e-06)
            gates = rx[3, :, rr, hh].reshape(TOK, DH).astype(F32)
            normed = full * scale * gain[:, hh] * (1.0 / (1.0 + jnp.exp(-gates)))
            abuf[0, :, rr, hh] = normed.astype(BF16).reshape(4, CH, DH)
        for i, d in enumerate(DELTAS):
            rr = pl.ds(j * CH, CH)
            send(
                abuf.at[0, :, rr, :], abuf.at[1 + i, :, rr, :],
                ag_s, ag_r.at[j], (at_x(d), z, p),
            )

    a2a_wait(2)
    local[6].wait()
    for j in range(4):
        inside(j)
    a2a_wait(3)
    arrived(st_in, st_sem.at[1])
    for j in range(4):
        finish(j)
    relays(0)

    xs = [lax.rem(x + d, 4) for d in (0, 3, 1, 2)]
    local[7].wait()

    def project(j):
        arrived(abuf.at[1:4, :, pl.ds(j * CH, CH), :], ag_r.at[j])
        if j == 0:
            arrived(wbuf.at[1], w_r.at[4])

        def body(n, carry):
            d = n + lax.div(n, 2)
            acc = jnp.zeros((4 * CH, NW), F32)
            for s in range(4):
                lhs = abuf[s, :, j * CH : (j + 1) * CH, :].reshape(4 * CH, HW)
                acc = acc + dot(lhs, wbuf[d, block(xs[s], HW), :])
            acc = acc.astype(BF16)
            yy = lax.rem(y + d, 4)
            part[j, 2 * yy] = acc[:SH, :]
            part[j, 2 * yy + 1] = acc[SH:, :]
            return carry

        lax.fori_loop(0, 3, body, 0)

    def project_late():
        arrived(wbuf.at[2], wr_r)
        yy = lax.rem(y + 2, 4)

        def body(n, carry):
            for i in range(2):
                acc = jnp.zeros((TOK, NW), F32)
                for s in range(4):
                    acc = acc + dot(abuf[s, 2 * n + i], wbuf[2, block(xs[s], HW), :])
                acc = acc.astype(BF16)
                for j in range(4):
                    part[j, 2 * yy + n, i * CH : (i + 1) * CH, :] = acc[j * CH : (j + 1) * CH, :]
            return carry

        lax.fori_loop(0, 2, body, 0)

    def owner(k):
        return lax.rem(z + k + 16, 8)

    def is_late(o):
        return lax.rem(lax.div(o, 2) - y + 4, 4) == 2

    def when(o, late):
        return pl.when(is_late(o) if late else jnp.logical_not(is_late(o)))

    def sign(j):
        return (1, -1)[j % 2]

    def long_copy(src, j, t):
        return remote(
            src, longs.at[j, t], l_s, l_r.at[j, t], (c, at_z(-sign(j)), p)
        )

    def short_copy(src, j, t):
        return remote(
            src, shorts.at[j, t], s_s, s_r.at[j, t], (c, at_z(sign(j)), p)
        )

    def start(j, late):
        s = sign(j)
        lo, so = owner(-4 * s), owner(3 * s)

        @when(lo, late)
        def _():
            long_copy(part.at[j, lo], j, 0).start()

        @when(so, late)
        def _():
            short_copy(part.at[j, so], j, 0).start()

    def fin_copy(j, i):
        return remote(
            total.at[j, pl.ds(i * CH, CH), :],
            out_hbm.at[0, pl.ds(j * CH, CH), block(lax.rem(x, 2), NW)],
            fin_s, fin_r, fin_dev(i),
        )

    def step(j, t, late):
        s = sign(j)
        lo, so = owner(-s * (3 - t)), owner(s * (2 - t))

        @when(lo, late)
        def _():
            arrived(longs.at[j, t], l_r.at[j, t])
            mine = longs[j, t].astype(F32) + part[j, lo].astype(F32)
            if t < 3:
                longs[j, t] = mine.astype(BF16)
                long_copy(longs.at[j, t], j, t + 1).start()
            else:
                arrived(shorts.at[j, 2], s_r.at[j, 2])
                total[j] = (mine + shorts[j, 2].astype(F32)).astype(BF16)
                for i in range(2):
                    fin_copy(j, i).start()

        if t < 2:

            @when(so, late)
            def _():
                arrived(shorts.at[j, t], s_r.at[j, t])
                mine = shorts[j, t].astype(F32) + part[j, so].astype(F32)
                shorts[j, t] = mine.astype(BF16)
                short_copy(shorts.at[j, t], j, t + 1).start()

    for op in ORDER:
        if op[0] == "S":
            project(op[1])
            start(op[1], False)
        elif op[0] == "L":
            project_late()
            for j in range(4):
                start(j, True)
        else:
            step(op[1], op[2], op[0] == "U")

    arrived(out_hbm.at[0], fin_r)
    all_sent(pkx.at[0:3], pk_s)
    all_sent(rx.at[0:3], a2a_s)
    all_sent(wbuf.at[0:2], w_s)
    all_sent(wbuf.at[2], wr_s)
    all_sent(st_out, st_sem.at[0])
    all_sent(abuf.at[0:3], ag_s)
    all_sent(longs, l_s)
    all_sent(shorts, s_s)
    all_sent(total, fin_s)


def on_device(queries, keys, values, gates, log_decay, segment_ids, norm_gain, out_weight):
    hbm = pl.BlockSpec(memory_space=pltpu.HBM)
    vmem = pltpu.VMEM
    dma = pltpu.SemaphoreType.DMA
    return pl.pallas_call(
        kernel,
        out_shape=jax.ShapeDtypeStruct((1, TOK, 2 * NW), BF16),
        in_specs=[hbm] * 8,
        out_specs=hbm,
        scratch_shapes=[
            vmem((4, 4, TOK, HW), BF16),
            vmem((16, TOK), F32),
            vmem((1, TOK), jnp.int32),
            vmem((1, HW), F32),
            vmem((4, 16, TOK), F32),
            vmem((4 * TOK, HW), BF16),
            vmem((4, TOK, HW), F32),
            vmem((4, 4, TOK, HW), BF16),
            vmem((4, KD, NW), BF16),
            vmem((272, DH), BF16),
            vmem((272, DH), BF16),
            vmem((4, 8, SH, NW), BF16),
            vmem((4, 4, SH, NW), BF16),
            vmem((4, 3, SH, NW), BF16),
            vmem((4, SH, NW), BF16),
            pltpu.SemaphoreType.REGULAR, dma((4,)), dma, dma((4,)), dma, dma,
            dma, dma((5,)), dma, dma, dma((2,)), dma, dma((4,)),
            dma, dma((4, 4)), dma, dma((4, 3)), dma, dma,
        ],
        compiler_params=pltpu.CompilerParams(
            collective_id=0, has_side_effects=True, vmem_limit_bytes=60 * 2**20
        ),
        cost_estimate=pl.CostEstimate(
            flops=2 * 10**9, bytes_accessed=3 * 2**20, transcendentals=10**6
        ),
    )(
        keys, values, queries, gates, log_decay[0].T, segment_ids, norm_gain, out_weight
    )


def solution(mesh):
    return jax.shard_map(
        on_device,
        mesh=mesh,
        in_specs=(
            P("pipe", "ctx", "head"),
            P("pipe", "ctx", "head"),
            P("pipe", "ctx", "head"),
            P("pipe", "ctx", "head"),
            P("pipe", "ctx", "head"),
            P("pipe", "ctx"),
            P("pipe", "head"),
            P("pipe", "head", "ctx"),
        ),
        out_specs=P("pipe", "ctx", "head"),
        check_vma=False,
    )
```

```python
import jax
import jax.numpy as jnp
from jax import lax
from jax.experimental import pallas as pl
from jax.experimental.pallas import tpu as pltpu
from jax.sharding import PartitionSpec as P

MESH = pl.DeviceIdType.MESH
F32 = jnp.float32
BF16 = jnp.bfloat16
HIGHEST = lax.Precision.HIGHEST

DH = 128
TOK = 128
HW = 256
KD = 1024
NW = 384
CH = 32
SH = 64
DELTAS = (1, 3, 2)
ORDER = (
    ("S", 0), ("S", 1), ("S", 2), ("S", 3), ("L",), ("T", 0, 0),
    ("U", 0, 0), ("T", 1, 0), ("U", 1, 0), ("T", 2, 0), ("U", 2, 0), ("T", 3, 0),
    ("U", 3, 0), ("T", 0, 1), ("U", 0, 1), ("T", 1, 1), ("U", 1, 1), ("T", 2, 1),
    ("U", 2, 1), ("T", 3, 1), ("U", 3, 1), ("T", 0, 2), ("U", 0, 2), ("T", 1, 2),
    ("U", 1, 2), ("T", 2, 2), ("U", 2, 2), ("T", 3, 2), ("U", 3, 2), ("T", 0, 3),
    ("U", 0, 3), ("T", 1, 3), ("U", 1, 3), ("T", 2, 3), ("U", 2, 3), ("T", 3, 3),
    ("U", 3, 3),
)


def dot(a, b, dims=((1,), (0,)), precision=None):
    return lax.dot_general(
        a, b, (dims, ((), ())), precision=precision, preferred_element_type=F32
    )


def kernel(
    k_hbm, v_hbm, q_hbm, g_hbm, decay_hbm, docs_hbm, gain_hbm, w_hbm, out_hbm,
    rx, pk, docs, gain, pkx, kf, att, abuf, wbuf, st_out, st_in,
    part, longs, shorts, total,
    go, lsem, a2a_s, a2a_r, pk_s, pk_r, w_s, w_r, wr_s, wr_r, st_sem,
    ag_s, ag_r, l_s, l_r, s_s, s_r, fin_s, fin_r,
):
    c, z, p = lax.axis_index("ctx"), lax.axis_index("head"), lax.axis_index("pipe")
    x, y = lax.rem(c, 4), lax.div(c, 4)

    def at_x(d):
        return 4 * y + lax.rem(x + d, 4)

    def at_y(d):
        return 4 * lax.rem(y + d, 4) + x

    def at_z(d):
        return lax.rem(z + d + 8, 8)

    def block(i, size):
        return pl.ds(pl.multiple_of(i * size, size), size)

    def remote(src, dst, send, recv, dev):
        return pltpu.make_async_remote_copy(
            src_ref=src, dst_ref=dst, send_sem=send, recv_sem=recv,
            device_id=dev, device_id_type=MESH,
        )

    def arrived(dst, recv):
        remote(dst, dst, recv, recv, (c, z, 1 - p)).wait_recv()

    def send(*a):
        remote(*a).start()

    def all_sent(ref, sem):
        remote(ref, ref, sem, sem, (c, z, 1 - p)).wait_send()

    local = [
        pltpu.make_async_copy(src, dst, a2a_r.at[i] if i < 4 else lsem.at[i - 4])
        for i, (src, dst) in enumerate(
            [
                (ref.at[0, :, block(x, HW)], rx.at[a, x])
                for a, ref in enumerate((k_hbm, v_hbm, q_hbm, g_hbm))
            ]
            + [
                (decay_hbm, pk.at[0:8, :]),
                (docs_hbm, docs),
                (gain_hbm.at[:, block(x, HW)], gain),
                (w_hbm.at[0], wbuf.at[0]),
            ]
        )
    ]
    for i in (4, 5, 6, 0, 1, 2, 3, 7):
        local[i].start()

    yo, half = lax.div(z, 2), lax.rem(z, 2)

    def fin_dev(i):
        return (4 * y + 2 * half + i, 2 * yo + lax.div(x, 2), 1 - p)

    barrier = pltpu.get_barrier_semaphore()
    peers = [(at_x(d), z, p) for d in DELTAS]
    peers += [(at_y(1), z, p), (at_y(3), z, p)]
    peers += [(c, at_z(1), p), (c, at_z(-1), p)]
    peers += [fin_dev(0), fin_dev(1)]
    peers.append((c, z, 1 - p))
    for dev in peers:
        pl.semaphore_signal(barrier, inc=1, device_id=dev, device_id_type=MESH)
    local[4].wait()
    local[5].wait()
    pk[8:16, :] = jnp.broadcast_to(docs[...].astype(F32), (8, TOK))
    pl.semaphore_wait(barrier, len(peers))

    for i, d in enumerate(DELTAS):
        send(pk, pkx.at[x], pk_s, pk_r, (at_x(d), z, p))

    def a2a(a, ref):
        for i, d in enumerate(DELTAS):
            to = lax.rem(x + d, 4)
            send(
                ref.at[0, :, block(to, HW)], rx.at[a, x],
                a2a_s, a2a_r.at[a], (at_x(d), z, p),
            )

    def a2a_wait(a):
        arrived(rx.at[a], a2a_r.at[a])

    def w_copy(side, ch):
        rows = pl.ds(ch * HW, HW)
        first = (ch < 2) == (side == 0)
        return remote(
            w_hbm.at[0, rows, :], wbuf.at[(3, 1)[side], rows, :],
            w_s, w_r.at[ch if first else 4], (at_y((1, 3)[side]), z, p),
        )

    def w_relay_copy(side, ch):
        rows = pl.ds(ch * HW, HW)
        return remote(
            wbuf.at[(3, 1)[side], rows, :], wbuf.at[2, rows, :],
            wr_s, wr_r, (at_y((1, 3)[side]), z, p),
        )

    def weights(core, chunks):
        @pl.when(p == core)
        def _():
            for side, ch in chunks:
                w_copy(side, ch).start()

    def relays(core):
        @pl.when(p == core)
        def _():
            for ch in range(2):
                for side, i in ((0, ch), (1, 2 + ch)):
                    arrived(wbuf.at[(3, 1)[side], pl.ds(i * HW, HW), :], w_r.at[i])
                    w_relay_copy(side, i).start()

    @pl.when(p == 0)
    def _():
        pl.semaphore_wait(go, 1)

    a2a(0, k_hbm)
    a2a(1, v_hbm)
    weights(1, ((0, 0), (1, 2), (0, 1), (1, 3)))
    @pl.when(p == 1)
    def _():
        a2a(2, q_hbm)
        a2a(3, g_hbm)

    weights(1, ((1, 0), (0, 2), (1, 1)))

    i8 = lax.broadcasted_iota(jnp.int32, (8, 8), 0)
    j8 = lax.broadcasted_iota(jnp.int32, (8, 8), 1)
    pick = (j8 == 2 * x + i8).astype(F32)
    ia = lax.broadcasted_iota(jnp.int32, (TOK, TOK), 0)
    ib = lax.broadcasted_iota(jnp.int32, (TOK, TOK), 1)
    upper = (ia <= ib).astype(F32)
    lower = (ia >= ib).astype(F32)
    eye = (ia == ib).astype(F32)
    arrived(pkx.at[0:3], pk_r)
    pkx[x] = pk[...]
    rows_, cols_, segr, segc = [], [], [], []
    off_r, off_c = jnp.zeros((8, 1), F32), jnp.zeros((1, 8), F32)
    for b in range(4):
        two = dot(pick, pkx[b, 0:8, :], precision=HIGHEST)
        r = dot(two, upper, precision=HIGHEST) + off_r
        s = dot(lower, two, ((1,), (1,)), precision=HIGHEST) + off_c
        e = dot(eye, pkx[b, 8:16, :], ((1,), (1,)), precision=HIGHEST)
        off_r, off_c = r[:, TOK - 1 : TOK], s[TOK - 1 : TOK, :]
        rows_.append(r)
        cols_.append(s)
        segr.append(pkx[b, 8:9, :])
        segc.append(e[:, 0:1])
    last_doc = segr[3][:, TOK - 1 : TOK]

    @pl.when(p == 0)
    def _():
        a2a(2, q_hbm)
        a2a(3, g_hbm)

    weights(0, ((1, 2), (1, 3)))
    a2a_wait(0)
    a2a_wait(1)

    @pl.when(p == 1)
    def _():
        pl.semaphore_signal(go, inc=1, device_id=(c, z, 0), device_id_type=MESH)

    for b in range(4):
        keep = (segc[b] == last_doc).astype(F32)
        for h in range(2):
            hs = slice(h, h + 1)
            hh = slice(h * DH, (h + 1) * DH)
            fade = jnp.exp(jnp.minimum(off_c[:, hs] - cols_[b][:, hs], 0.0)) * keep
            kf[b * TOK : (b + 1) * TOK, hh] = (rx[0, b, :, hh].astype(F32) * fade).astype(BF16)
    for h in range(2):
        hh = slice(h * DH, (h + 1) * DH)
        values = rx[1, :, :, hh].reshape(4 * TOK, DH)
        st_out[hh, :] = dot(kf[:, hh], values, ((0,), (0,))).astype(BF16)
    st_out[256:272, :] = jnp.broadcast_to(last_doc, (16, DH)).astype(BF16)
    send(st_out, st_in, st_sem.at[0], st_sem.at[1], (at_y(1), z, p))
    weights(1, ((0, 3),))
    weights(0, ((0, 0), (0, 1), (0, 2), (1, 0), (0, 3), (1, 1)))

    base = lax.broadcasted_iota(jnp.int32, (TOK, 4 * TOK), 0)
    base = lax.shift_right_logical(base, 5) * TOK + (base & (CH - 1))
    ahead = lax.broadcasted_iota(jnp.int32, (TOK, 4 * TOK), 1) - base
    seg_row = jnp.concatenate(segr, axis=1)
    crow = [jnp.concatenate([r[h : h + 1, :] for r in rows_], axis=1) for h in range(2)]
    later = (y > 0).astype(F32)

    def inside(j):
        rr = slice(j * CH, (j + 1) * CH)
        seg_t = jnp.concatenate([e[rr, :] for e in segc], axis=0)
        allowed = (ahead <= j * CH) & (seg_t == seg_row)
        for h in range(2):
            hh = slice(h * DH, (h + 1) * DH)
            ccol = jnp.concatenate([s[rr, h : h + 1] for s in cols_], axis=0)
            weight = jnp.where(allowed, jnp.exp(jnp.minimum(ccol - crow[h], 0.0)), 0.0)
            queries = rx[2, :, rr, hh].reshape(TOK, DH)
            scores = dot(queries, rx[0, :, :, hh].reshape(4 * TOK, DH), ((1,), (1,)))
            mixed = (scores * weight).astype(BF16)
            att[j, :, hh] = dot(mixed, rx[1, :, :, hh].reshape(4 * TOK, DH))

    def finish(j):
        rr = slice(j * CH, (j + 1) * CH)
        prev_doc = st_in[256:257, 0:1].astype(F32)
        seg_t = jnp.concatenate([e[rr, :] for e in segc], axis=0)
        same = (seg_t == prev_doc).astype(F32) * later
        for h in range(2):
            hh = slice(h * DH, (h + 1) * DH)
            ccol = jnp.concatenate([s[rr, h : h + 1] for s in cols_], axis=0)
            queries = rx[2, :, rr, hh].reshape(TOK, DH)
            full = att[j, :, hh] + dot(queries, st_in[hh, :]) * (jnp.exp(ccol) * same)
            scale = lax.rsqrt(jnp.mean(full * full, axis=-1, keepdims=True) + 1e-06)
            gates = rx[3, :, rr, hh].reshape(TOK, DH).astype(F32)
            normed = full * scale * gain[:, hh] * (1.0 / (1.0 + jnp.exp(-gates)))
            abuf[0, :, rr, hh] = normed.astype(BF16).reshape(4, CH, DH)
        for i, d in enumerate(DELTAS):
            rr = pl.ds(j * CH, CH)
            send(
                abuf.at[0, :, rr, :], abuf.at[1 + i, :, rr, :],
                ag_s, ag_r.at[j], (at_x(d), z, p),
            )

    a2a_wait(2)
    local[6].wait()
    for j in range(4):
        inside(j)
    relays(1)
    a2a_wait(3)
    arrived(st_in, st_sem.at[1])
    for j in range(4):
        finish(j)
    relays(0)

    xs = [lax.rem(x + d, 4) for d in (0, 3, 1, 2)]
    local[7].wait()

    def project(j):
        arrived(abuf.at[1:4, :, pl.ds(j * CH, CH), :], ag_r.at[j])
        if j == 0:
            arrived(wbuf.at[1], w_r.at[4])

        def body(n, carry):
            d = n + lax.div(n, 2)
            acc = jnp.zeros((4 * CH, NW), F32)
            for s in range(4):
                lhs = abuf[s, :, j * CH : (j + 1) * CH, :].reshape(4 * CH, HW)
                acc = acc + dot(lhs, wbuf[d, block(xs[s], HW), :])
            acc = acc.astype(BF16)
            yy = lax.rem(y + d, 4)
            part[j, 2 * yy] = acc[:SH, :]
            part[j, 2 * yy + 1] = acc[SH:, :]
            return carry

        lax.fori_loop(0, 3, body, 0)

    def project_late():
        arrived(wbuf.at[2], wr_r)
        yy = lax.rem(y + 2, 4)

        def body(n, carry):
            for i in range(2):
                acc = jnp.zeros((TOK, NW), F32)
                for s in range(4):
                    acc = acc + dot(abuf[s, 2 * n + i], wbuf[2, block(xs[s], HW), :])
                acc = acc.astype(BF16)
                for j in range(4):
                    part[j, 2 * yy + n, i * CH : (i + 1) * CH, :] = acc[j * CH : (j + 1) * CH, :]
            return carry

        lax.fori_loop(0, 2, body, 0)

    def owner(k):
        return lax.rem(z + k + 16, 8)

    def is_late(o):
        return lax.rem(lax.div(o, 2) - y + 4, 4) == 2

    def when(o, late):
        return pl.when(is_late(o) if late else jnp.logical_not(is_late(o)))

    def sign(j):
        return (1, -1)[j % 2]

    def long_copy(src, j, t):
        return remote(
            src, longs.at[j, t], l_s, l_r.at[j, t], (c, at_z(-sign(j)), p)
        )

    def short_copy(src, j, t):
        return remote(
            src, shorts.at[j, t], s_s, s_r.at[j, t], (c, at_z(sign(j)), p)
        )

    def start(j, late):
        s = sign(j)
        lo, so = owner(-4 * s), owner(3 * s)

        @when(lo, late)
        def _():
            long_copy(part.at[j, lo], j, 0).start()

        @when(so, late)
        def _():
            short_copy(part.at[j, so], j, 0).start()

    def fin_copy(j, i):
        return remote(
            total.at[j, pl.ds(i * CH, CH), :],
            out_hbm.at[0, pl.ds(j * CH, CH), block(lax.rem(x, 2), NW)],
            fin_s, fin_r, fin_dev(i),
        )

    def step(j, t, late):
        s = sign(j)
        lo, so = owner(-s * (3 - t)), owner(s * (2 - t))

        @when(lo, late)
        def _():
            arrived(longs.at[j, t], l_r.at[j, t])
            mine = longs[j, t].astype(F32) + part[j, lo].astype(F32)
            if t < 3:
                longs[j, t] = mine.astype(BF16)
                long_copy(longs.at[j, t], j, t + 1).start()
            else:
                arrived(shorts.at[j, 2], s_r.at[j, 2])
                total[j] = (mine + shorts[j, 2].astype(F32)).astype(BF16)
                for i in range(2):
                    fin_copy(j, i).start()

        if t < 2:

            @when(so, late)
            def _():
                arrived(shorts.at[j, t], s_r.at[j, t])
                mine = shorts[j, t].astype(F32) + part[j, so].astype(F32)
                shorts[j, t] = mine.astype(BF16)
                short_copy(shorts.at[j, t], j, t + 1).start()

    for op in ORDER:
        if op[0] == "S":
            project(op[1])
            start(op[1], False)
        elif op[0] == "L":
            project_late()
            for j in range(4):
                start(j, True)
        else:
            step(op[1], op[2], op[0] == "U")

    arrived(out_hbm.at[0], fin_r)
    all_sent(pkx.at[0:3], pk_s)
    all_sent(rx.at[0:3], a2a_s)
    all_sent(wbuf.at[0:2], w_s)
    all_sent(wbuf.at[2], wr_s)
    all_sent(st_out, st_sem.at[0])
    all_sent(abuf.at[0:3], ag_s)
    all_sent(longs, l_s)
    all_sent(shorts, s_s)
    all_sent(total, fin_s)


def on_device(queries, keys, values, gates, log_decay, segment_ids, norm_gain, out_weight):
    hbm = pl.BlockSpec(memory_space=pltpu.HBM)
    vmem = pltpu.VMEM
    dma = pltpu.SemaphoreType.DMA
    return pl.pallas_call(
        kernel,
        out_shape=jax.ShapeDtypeStruct((1, TOK, 2 * NW), BF16),
        in_specs=[hbm] * 8,
        out_specs=hbm,
        scratch_shapes=[
            vmem((4, 4, TOK, HW), BF16),
            vmem((16, TOK), F32),
            vmem((1, TOK), jnp.int32),
            vmem((1, HW), F32),
            vmem((4, 16, TOK), F32),
            vmem((4 * TOK, HW), BF16),
            vmem((4, TOK, HW), F32),
            vmem((4, 4, TOK, HW), BF16),
            vmem((4, KD, NW), BF16),
            vmem((272, DH), BF16),
            vmem((272, DH), BF16),
            vmem((4, 8, SH, NW), BF16),
            vmem((4, 4, SH, NW), BF16),
            vmem((4, 3, SH, NW), BF16),
            vmem((4, SH, NW), BF16),
            pltpu.SemaphoreType.REGULAR, dma((4,)), dma, dma((4,)), dma, dma,
            dma, dma((5,)), dma, dma, dma((2,)), dma, dma((4,)),
            dma, dma((4, 4)), dma, dma((4, 3)), dma, dma,
        ],
        compiler_params=pltpu.CompilerParams(
            collective_id=0, has_side_effects=True, vmem_limit_bytes=60 * 2**20
        ),
        cost_estimate=pl.CostEstimate(
            flops=2 * 10**9, bytes_accessed=3 * 2**20, transcendentals=10**6
        ),
    )(
        keys, values, queries, gates, log_decay[0].T, segment_ids, norm_gain, out_weight
    )


def solution(mesh):
    return jax.shard_map(
        on_device,
        mesh=mesh,
        in_specs=(
            P("pipe", "ctx", "head"),
            P("pipe", "ctx", "head"),
            P("pipe", "ctx", "head"),
            P("pipe", "ctx", "head"),
            P("pipe", "ctx", "head"),
            P("pipe", "ctx"),
            P("pipe", "head"),
            P("pipe", "head", "ctx"),
        ),
        out_specs=P("pipe", "ctx", "head"),
        check_vma=False,
    )
```
